512 devices in a mesh: seq: 64 (over y, z_lo, core), tp: 8 (over z_hi, x).
Axes of the slice: x: 4, y: 8, z: 8 (z_hi: 2, z_lo: 4; z = z_hi * 4 + z_lo), core: 2. Of those that a mesh axis runs over, the one named last changes fastest.
Arguments:
- frames_in: bfloat16 [16384, 1024], P('seq'), may hold values from -6 to 6
- stretch_map: int32 [64, 64], replicated, may hold values from 0 to 63, as said below
- rec_lengths: int32 [8], replicated, may hold values from 1 to 4096, 16384 in all
- windows: int32 [8], replicated, may hold values from 32 to 128
- ln1_gain: float32 [1024], replicated, may hold values from 0.6 to 5.5
- wqkv: bfloat16 [3, 1024, 1024], P(None, None, 'tp'), may hold values from -0.1875 to 0.1875
- wo: bfloat16 [1024, 1024], P('tp'), may hold values from -0.1875 to 0.1875
- ln2_gain: float32 [1024], replicated, may hold values from 0.5 to 1.5
- w1: bfloat16 [2, 1024, 1024], P(None, None, 'tp'), may hold values from -0.1875 to 0.1875
- dw_kernel: float32 [9, 1024], P(None, 'tp'), may hold values from -6 to 6
- bn_scale: float32 [1024], P('tp'), may hold values from 0.5 to 2
- bn_shift: float32 [1024], P('tp'), may hold values from -3 to 3
- w2: bfloat16 [1024, 1024], P('tp'), may hold values from -0.1875 to 0.1875
Outputs:
- block_out: bfloat16 [16384, 1024], P('seq', 'tp')
The draws below stay inside these ranges and needn't reach their ends.
Inputs may be any that keep to these rules, and one draw needn't show every extreme that they name: Every column of stretch_map holds each of 0 to 63 exactly once. `rec_lengths`: the lengths sum to 16384.
All inputs are finite; a program needn't handle non-finite values.
Results may differ from the reference program's by a relative error of at most 0.023.
The reference program's roundings to bfloat16 on the way count: a program that leaves them out, or rounds other values in their place, can miss the bound.
Values may be sent and summed in bfloat16 or wider, within the bound.
A program may use at most 64 MiB of HBM per device.

```python
import math
import jax
import jax.numpy as jnp
import numpy as np
from jax import lax

D = 1024
H = 8
HD = 128
FRAMES_DEV = 256
WMAX = 128
KERNEL = 9
RECS = 8
SHARDS = 64
PIECE = 4
FRAMES = 16384
N_TP = 8


def shuffle_column(sub_key):
    return jax.random.permutation(sub_key, SHARDS).astype(jnp.int32)


def draw_stretch_map(key, part):
    key = jax.random.fold_in(key, 11)
    column_keys = jax.random.split(key, SHARDS)
    columns = jax.vmap(shuffle_column)(column_keys)
    return jnp.transpose(columns)


def draw_windows(key, part):
    key = jax.random.fold_in(key, 12)
    base = jax.random.randint(key, (RECS,), WMAX // 4, WMAX + 1).astype(jnp.int32)
    picks = jax.random.permutation(jax.random.fold_in(key, 5), RECS)
    base = base.at[picks[0]].set(WMAX)
    return base.at[picks[1]].set(WMAX // 4)


def draw_ln1_gain(key, part):
    key = jax.random.fold_in(key, 13)
    return jax.random.uniform(key, (D,), jnp.float32, 0.6, 2.0)


def levels(key, extent, cuts, least, high):
    factor_of = 1.0
    for position, blocks in cuts:
        heights = jax.random.uniform(jax.random.fold_in(jax.random.fold_in(key, 6), position), (blocks,), jnp.float32, least / len(cuts), high / len(cuts))
        factor_of = factor_of * jnp.repeat(jnp.exp(heights), extent[position] // blocks).reshape((-1,) + (1,) * (len(extent) - 1 - position))
    return factor_of


def length_profile(amount, total, most, lean):
    portions = [(1 << 20) // math.isqrt(standing ** lean) + 1 for standing in range(2, amount + 1)]
    surplus, given = total - most - (amount - 1), [1] * (amount - 1)
    while surplus > 0:
        candidates = [i for i in range(amount - 1) if given[i] < most]
        mass, remaining = sum([portions[i] for i in candidates]), surplus
        for i in candidates:
            addition = min(most - given[i], max(1, remaining * portions[i] // mass), surplus)
            given[i] = given[i] + addition
            surplus = surplus - addition
    return np.array([most] + given)


def uneven_parts(key, amount, total, most, lean):
    if amount == 2:
        one = jax.random.randint(key, (), max(1, total - most), min(most, total - 1) + 1)
        return jnp.stack([one, total - one])
    sizes = jnp.asarray(length_profile(amount, total, most, lean), jnp.int32)
    pairs = (amount - 1) // 2
    source_of, sink = sizes[1:1 + 2 * pairs:2], sizes[2:2 + 2 * pairs:2]
    slack = jnp.minimum(source_of - 1, most - sink)
    shifted = jax.random.randint(jax.random.fold_in(key, 1), (pairs,), 0, 1 << 20) % (slack + 1)
    sizes = sizes.at[1:1 + 2 * pairs:2].set(source_of - shifted).at[2:2 + 2 * pairs:2].set(sink + shifted)
    return sizes[jax.random.permutation(jax.random.fold_in(key, 2), amount)]


def scatter_about(stream_key, shape, width, most, shards=(), held_as=jnp.bfloat16):
    drawn = width * jax.random.normal(stream_key, shape, jnp.float32)
    if shards:
        drawn = drawn * levels(stream_key, shape, shards, -0.22, 0.18)
    return jnp.clip(drawn, -most, most).astype(held_as)


def setup_inputs(seed: int = 0) -> dict:
    streams_of = jax.random.split(jax.random.key(seed), 14)
    frames_in = scatter_about(streams_of[0], (FRAMES, D), 1.0, 6.0, ((0, 64),))
    stretch_map = draw_stretch_map(jax.random.fold_in(streams_of[13], 71), 0)
    rec_lengths = uneven_parts(streams_of[2], RECS, FRAMES, FRAMES // 4, 2).astype(jnp.int32)
    windows = draw_windows(jax.random.fold_in(streams_of[13], 71), 0)
    ln1_gain = draw_ln1_gain(jax.random.fold_in(streams_of[13], 71), 0)
    wqkv = scatter_about(streams_of[5], (3, D, D), D ** -0.5, 0.1875, ((2, 8),))
    wo = scatter_about(streams_of[6], (D, D), D ** -0.5, 0.1875, ((0, 8),))
    ln2_gain = jnp.clip(1.0 + 0.1 * jax.random.normal(streams_of[7], (D,), jnp.float32), 0.5, 1.5)
    w1 = scatter_about(streams_of[8], (2, D, D), D ** -0.5, 0.1875, ((2, 8),))
    dw_kernel = scatter_about(streams_of[9], (KERNEL, D), 1 ** -0.5, 6.0, ((1, 8),), jnp.float32)
    bn_scale = jnp.clip(jnp.exp(math.log(2.0) - 1.3862944 * jax.random.uniform(streams_of[10], (D,), jnp.float32) ** levels(streams_of[10], (D,), ((0, 8),), -0.2, 0.2)), 0.5, 2.0)
    bn_shift = scatter_about(streams_of[11], (D,), 0.5, 3.0, ((0, 8),), jnp.float32)
    w2 = scatter_about(streams_of[12], (D, D), D ** -0.5, 0.1875, ((0, 8),))
    return {"frames_in": frames_in, "stretch_map": stretch_map, "rec_lengths": rec_lengths, "windows": windows, "ln1_gain": ln1_gain, "wqkv": wqkv, "wo": wo, "ln2_gain": ln2_gain, "w1": w1, "dw_kernel": dw_kernel, "bn_scale": bn_scale, "bn_shift": bn_shift, "w2": w2}


def layer_norm(values, gain_vector):
    wide = values.astype(jnp.float32)
    row_mean = lax.optimization_barrier(jnp.mean(wide, axis=-1, keepdims=True))
    centred = wide - row_mean
    row_var = lax.optimization_barrier(jnp.mean(centred * centred, axis=-1, keepdims=True))
    return centred * lax.rsqrt(row_var + 1e-05) * gain_vector

def recording_ids(positions, rec_ends):
    return lax.optimization_barrier(jnp.sum((positions[:, None] >= rec_ends[None, :]).astype(jnp.int32), axis=1))

def allowed_pairs(query_pos, key_pos, rec_ends, windows, total):
    query_rec = recording_ids(query_pos, rec_ends)
    key_rec = recording_ids(key_pos, rec_ends)
    hits = query_rec[:, None] == jnp.arange(windows.shape[0], dtype=jnp.int32)[None, :]
    query_window = lax.optimization_barrier(jnp.sum(jnp.where(hits, windows[None, :], 0), axis=1))
    inside = (key_pos >= 0) & (key_pos < total)
    same = query_rec[:, None] == key_rec[None, :]
    near = jnp.abs(query_pos[:, None] - key_pos[None, :]) <= query_window[:, None]
    return inside[None, :] & same & near

def grouped_sum(left, right):
    group = D // N_TP
    total_sum = jnp.zeros((left.shape[0], right.shape[1]), jnp.float32)
    for index in range(N_TP):
        term = jnp.dot(left[:, index * group:(index + 1) * group], right[index * group:(index + 1) * group], preferred_element_type=jnp.float32).astype(jnp.bfloat16)
        term = lax.optimization_barrier(term)
        total_sum = total_sum + term.astype(jnp.float32)
    return total_sum

def reference(frames_in, stretch_map, rec_lengths, windows, ln1_gain, wqkv, wo, ln2_gain, w1, dw_kernel, bn_scale, bn_shift, w2):
    shard_count = SHARDS
    blocks = jnp.swapaxes(frames_in.reshape(shard_count, shard_count, PIECE, D), 0, 1)
    source_idx = jnp.broadcast_to(jnp.arange(shard_count, dtype=jnp.int32)[:, None], (shard_count, shard_count))
    block_idx = jnp.broadcast_to(jnp.arange(shard_count, dtype=jnp.int32)[None, :], (shard_count, shard_count))
    inverse = jnp.zeros((shard_count, shard_count), jnp.int32).at[block_idx, stretch_map].set(source_idx)
    ordered = jnp.take_along_axis(blocks, inverse[:, :, None, None], axis=1).reshape(FRAMES, D)
    z1 = layer_norm(ordered, ln1_gain).astype(jnp.bfloat16)
    queries = jnp.dot(z1, wqkv[0], preferred_element_type=jnp.float32).astype(jnp.bfloat16)
    keys_all = jnp.dot(z1, wqkv[1], preferred_element_type=jnp.float32).astype(jnp.bfloat16)
    values_all = jnp.dot(z1, wqkv[2], preferred_element_type=jnp.float32).astype(jnp.bfloat16)
    keys_pad = jnp.pad(keys_all, ((WMAX, WMAX), (0, 0)))
    values_pad = jnp.pad(values_all, ((WMAX, WMAX), (0, 0)))
    rec_ends = jnp.cumsum(rec_lengths).astype(jnp.int32)
    scale = 1.0 / math.sqrt(HD)
    block_rows = min(512, FRAMES_DEV)
    span = block_rows + 2 * WMAX

    def attend_block(block_index):
        start = (block_index * block_rows).astype(jnp.int32)
        query_blk = lax.dynamic_slice_in_dim(queries, start, block_rows, 0).reshape(block_rows, H, HD)
        key_blk = lax.dynamic_slice_in_dim(keys_pad, start, span, 0).reshape(span, H, HD)
        value_blk = lax.dynamic_slice_in_dim(values_pad, start, span, 0).reshape(span, H, HD)
        query_pos = start + jnp.arange(block_rows, dtype=jnp.int32)
        key_pos = start - WMAX + jnp.arange(span, dtype=jnp.int32)
        usable = allowed_pairs(query_pos, key_pos, rec_ends, windows, FRAMES)
        scores = jnp.einsum('qhd,khd->hqk', query_blk.astype(jnp.float32), key_blk.astype(jnp.float32)) * scale
        scores = jnp.where(usable, scores, -1e+30)
        row_max = lax.optimization_barrier(jnp.max(scores, axis=-1, keepdims=True))
        exp_scores = jnp.exp(scores - row_max)
        row_total = lax.optimization_barrier(jnp.sum(exp_scores, axis=-1, keepdims=True))
        probs = (exp_scores / row_total).astype(jnp.bfloat16)
        context = jnp.einsum('hqk,khd->qhd', probs.astype(jnp.float32), value_blk.astype(jnp.float32))
        return context.astype(jnp.bfloat16).reshape(block_rows, D)
    context = lax.map(attend_block, jnp.arange(FRAMES // block_rows, dtype=jnp.int32)).reshape(FRAMES, D)
    resid = (ordered.astype(jnp.float32) + grouped_sum(context, wo)).astype(jnp.bfloat16)
    z2 = layer_norm(resid, ln2_gain).astype(jnp.bfloat16)
    value_half = jnp.dot(z2, w1[0], preferred_element_type=jnp.float32)
    gate_half = jnp.dot(z2, w1[1], preferred_element_type=jnp.float32)
    glu = (value_half * jax.nn.sigmoid(gate_half)).astype(jnp.bfloat16)
    rim = (KERNEL - 1) // 2
    padded = jnp.pad(glu, ((rim, rim), (0, 0)))
    positions = jnp.arange(FRAMES, dtype=jnp.int32)
    own_rec = recording_ids(positions, rec_ends)
    running = jnp.zeros((FRAMES, D), jnp.float32)
    for offset in range(KERNEL):
        neighbour = positions + offset - rim
        usable = (neighbour >= 0) & (neighbour < FRAMES) & (recording_ids(neighbour, rec_ends) == own_rec)
        running = running + jnp.where(usable[:, None], padded[offset:offset + FRAMES].astype(jnp.float32) * dw_kernel[offset], 0.0)
    normed = running * bn_scale + bn_shift
    act = (normed * jax.nn.sigmoid(normed)).astype(jnp.bfloat16)
    return (resid.astype(jnp.float32) + grouped_sum(act, w2)).astype(jnp.bfloat16)
```

```python
import functools
import math

import jax
import jax.numpy as jnp
from jax import lax
from jax.experimental import pallas as pl
from jax.experimental.pallas import tpu as pltpu
from jax.sharding import PartitionSpec as P

MESH = pl.DeviceIdType.MESH
BF16 = jnp.bfloat16
F32 = jnp.float32
I32 = jnp.int32

SEQ = 64
TP = 8
NX = 4
ROWS = 256
HALF = 128
D = 1024
LW = 128
PIECE = 4
MSG = 16
WMAX = 128
TAPS = 9
RIM = 4
EDGE = 16


def dot(a, b):
    return jnp.dot(a, b, preferred_element_type=F32)


def dot_nt(a, b):
    return lax.dot_general(a, b, (((1,), (1,)), ((), ())), preferred_element_type=F32)


def iota(shape, dim):
    return lax.broadcasted_iota(I32, shape, dim)


def one_hot(mask):
    return jnp.where(mask, 1.0, 0.0).astype(BF16)


def layer_norm(blocks, gain_ref):
    width = blocks[0].shape[1]
    mean = sum(jnp.sum(b, axis=1, keepdims=True) for b in blocks) * (1.0 / D)
    centred = [b - mean for b in blocks]
    var = sum(jnp.sum(c * c, axis=1, keepdims=True) for c in centred) * (1.0 / D)
    inv = lax.rsqrt(var + 1e-05)
    normed = [
        (c * inv * gain_ref[:, i * width : (i + 1) * width]).astype(BF16)
        for i, c in enumerate(centred)
    ]
    return jnp.concatenate(normed, axis=1)


def block_kernel(
    frames, smap, lens, wins, gain1, wqkv, wo, gain2, w1, taps, bn_scale, bn_shift, w2,
    out,
    xin, sbuf, rbuf, frame, wq, wkv, w1v, wof, w2c, qv, kvx, ctx, act, res, glu, gluf, rim,
    lo_ref, hi_ref, start_ref, end_ref,
    ld, own_sem, a2a_s, a2a_r, xs, xr, hs, hr, wos, wor, w2s, w2r, c1s, c1r, c2s, c2r, gs, gr,
):
    s = lax.axis_index("seq")
    t = lax.axis_index("tp")
    z = t // NX
    x = lax.rem(t, NX)
    core = lax.rem(s, 2)
    mate = s + 1 - 2 * core
    left = lax.rem(s + SEQ - 1, SEQ)
    right = lax.rem(s + 1, SEQ)
    z_peer = lax.rem(t + NX, TP)

    def x_peer(d):
        return z * NX + lax.rem(x + d, NX)

    def remote(src, dst, send, recv, seq, tp):
        return pltpu.make_async_remote_copy(
            src_ref=src, dst_ref=dst, send_sem=send, recv_sem=recv,
            device_id=(seq, tp), device_id_type=MESH,
        )

    bar = pltpu.get_barrier_semaphore()

    def greet(d, carry):
        pl.semaphore_signal(bar, inc=1, device_id=(lax.rem(s + d, SEQ), t), device_id_type=MESH)
        return carry

    for d in range(1, TP):
        pl.semaphore_signal(bar, inc=1, device_id=(s, lax.rem(t + d, TP)), device_id_type=MESH)
    lax.fori_loop(1, SEQ, greet, 0)

    parity = lax.rem(x, 2)
    quarter = 2 * parity + x // 2
    loads = []

    def load(src, dst):
        cp = pltpu.make_async_copy(src, dst, ld.at[len(loads)])
        cp.start()
        loads.append(cp)
        return cp

    ld_frames = load(frames.at[:, pl.ds(pl.multiple_of(parity * 512, 512), 512)], xin)
    ld_wo = load(wo, wof.at[pl.ds(pl.multiple_of(t * LW, LW), LW)])
    ld_qkv = [
        load(wqkv.at[1], wkv.at[:, 0:LW]),
        load(wqkv.at[2], wkv.at[:, LW : 2 * LW]),
        load(wqkv.at[0], wq),
    ]
    ld_w1 = [load(w1.at[0], w1v.at[:, 0:LW]), load(w1.at[1], w1v.at[:, LW : 2 * LW])]
    ld_w2 = load(
        w2.at[:, pl.ds(pl.multiple_of(t * LW, LW), LW)],
        w2c.at[pl.ds(pl.multiple_of(t * LW, LW), LW)],
    )

    ld_frames.wait()
    o = iota((256, 256), 0)
    i = iota((256, 256), 1)
    pack = one_hot(i == 64 * ((o >> 2) & 3) + 4 * (o >> 4) + (o & 3))
    unpack = one_hot(o == 64 * ((i >> 2) & 3) + 4 * (i >> 4) + (i & 3))
    for g in range(4):
        stack = jnp.concatenate(
            [xin[64 * g : 64 * g + 64, 128 * c : 128 * c + 128] for c in range(4)], axis=0
        )
        sbuf[256 * g : 256 * g + 256, :] = dot(pack, stack).astype(BF16)

    pl.semaphore_wait(bar, SEQ - 1 + TP - 1)

    def rows16(index):
        return pl.ds(pl.multiple_of(index * MSG, MSG), MSG)

    def deal(d, carry):
        j = lax.rem(s + d, SEQ)
        remote(sbuf.at[rows16(j)], rbuf.at[rows16(s)], a2a_s, a2a_r, j, t).start()
        return carry

    lax.fori_loop(1, SEQ, deal, 0)
    own = pltpu.make_async_copy(sbuf.at[rows16(s)], rbuf.at[rows16(s)], own_sem)
    own.start()

    def wo_rows(tp, c):
        return wof.at[pl.ds(pl.multiple_of(tp * LW + c * 64, 64), 64)]

    ld_wo.wait()
    wo_first = []
    for k, peer in enumerate([x_peer(1), x_peer(2), x_peer(3), z_peer]):
        cp = remote(wo_rows(t, core), wo_rows(t, core), wos.at[k], wor.at[k], s, peer)
        cp.start()
        wo_first.append(cp)
    w2_first = []
    for k in range(1, TP):
        peer = lax.rem(t + k, TP)
        cp = remote(
            w2.at[pl.ds(pl.multiple_of(core * 64, 64), 64), pl.ds(pl.multiple_of(peer * LW, LW), LW)],
            w2c.at[pl.ds(pl.multiple_of(t * LW + core * 64, 64), 64)],
            w2s.at[k - 1], w2r.at[k - 1], s, peer,
        )
        cp.start()
        w2_first.append(cp)

    col = dot_nt(one_hot(iota((8, SEQ), 1) == s), smap[...].astype(F32).astype(BF16))
    spread = one_hot((iota((SEQ, 256), 1) >> 2) == iota((SEQ, 256), 0))
    place = dot(col.astype(BF16), spread) * 4.0 + (iota((8, 256), 1) & 3).astype(F32)
    order = one_hot(place[0:1, :] == o.astype(F32))

    pos = s * ROWS + iota((ROWS, LW), 0)
    start = jnp.zeros((ROWS, LW), I32)
    end = jnp.full((ROWS, LW), SEQ * ROWS, I32)
    reach = jnp.zeros((ROWS, LW), I32)
    total = jnp.int32(0)
    for k in range(8):
        before = total
        total = total + lens[k]
        start = jnp.where(pos >= total, total, start)
        end = jnp.where(pos < total, jnp.minimum(end, total), end)
        reach = jnp.where((pos >= before) & (pos < total), wins[k], reach)
    start_ref[...] = start
    end_ref[...] = end
    lo_ref[...] = jnp.maximum(start, pos - reach)
    hi_ref[...] = jnp.minimum(end - 1, pos + reach)

    own.wait()
    wait_all = remote(
        sbuf.at[0 : MSG * (SEQ - 1)], rbuf.at[0 : MSG * (SEQ - 1)], a2a_s, a2a_r, right, t
    )
    wait_all.wait_recv()
    parts = [dot(unpack, rbuf[256 * g : 256 * g + 256, :]).astype(BF16) for g in range(4)]
    dealt = jnp.concatenate(
        [
            jnp.concatenate([parts[g][64 * c : 64 * c + 64] for g in range(4)], axis=0)
            for c in range(4)
        ],
        axis=1,
    )
    ordered = dot(order, dealt).astype(BF16)
    frame[2 * parity] = ordered[:, 0:256]
    frame[2 * parity + 1] = ordered[:, 256:512]

    swaps = []
    for c in range(2):
        pair = []
        for n, d in enumerate((1, 3)):
            part = frame.at[quarter, c * HALF : (c + 1) * HALF]
            cp = remote(part, part, xs.at[c, n], xr.at[c, n], s, x_peer(d))
            cp.start()
            pair.append(cp)
        swaps.append(pair)

    for cp in ld_qkv:
        cp.wait()
    halos = []
    for c in range(2):
        for cp in swaps[c]:
            cp.wait_recv()
        rows = slice(c * HALF, (c + 1) * HALF)
        z1 = layer_norm([frame[q, rows, :].astype(F32) for q in range(4)], gain1)
        kvx[WMAX + c * HALF : WMAX + (c + 1) * HALF, :] = dot(z1, wkv[...]).astype(BF16)
        src = kvx.at[WMAX + c * HALF : WMAX + (c + 1) * HALF]
        if c == 0:
            cp = remote(src, kvx.at[WMAX + ROWS : 2 * WMAX + ROWS], hs.at[0], hr.at[0], left, t)
        else:
            cp = remote(src, kvx.at[0:WMAX], hs.at[1], hr.at[1], right, t)
        cp.start()
        halos.append(cp)
        qv[rows, :] = dot(z1, wq[...]).astype(BF16)

    wo_first[3].wait_recv()
    wo_next = []
    for d in range(1, NX):
        cp = remote(
            wo_rows(z_peer, core), wo_rows(z_peer, core), wos.at[3 + d], wor.at[3 + d], s, x_peer(d)
        )
        cp.start()
        wo_next.append(cp)
    wo_swap = []

    def give_wo(tp):
        k = 7 + len(wo_swap)
        cp = remote(wo_rows(tp, core), wo_rows(tp, core), wos.at[k], wor.at[k], mate, t)
        cp.start()
        wo_swap.append(cp)

    give_wo(z_peer)
    for d in range(1, NX):
        wo_first[d - 1].wait_recv()
        give_wo(x_peer(NX - d))

    def send_group(buf, rows, send, recv):
        sent = []
        for k, peer in enumerate([z_peer, x_peer(1), x_peer(2), x_peer(3)]):
            cp = remote(buf.at[t, rows], buf.at[t, rows], send.at[k], recv.at[k], s, peer)
            cp.start()
            sent.append(cp)
        return sent

    def pass_on(buf, rows, send, recv, sent):
        sent[0].wait_recv()
        for d in range(1, NX):
            cp = remote(
                buf.at[z_peer, rows], buf.at[z_peer, rows], send.at[3 + d], recv.at[3 + d],
                s, x_peer(d),
            )
            cp.start()
            sent.append(cp)

    def whole(buf, rows, sent):
        for cp in sent[1:]:
            cp.wait_recv()
        return jnp.concatenate([buf[k, rows, :] for k in range(TP)], axis=1)

    scale = 1.0 / math.sqrt(LW)
    sent1 = {}
    for c in (1, 0):
        rows = slice(c * HALF, (c + 1) * HALF)
        keys = slice(c * HALF, c * HALF + HALF + 2 * WMAX)
        halos[1 - c].wait_recv()
        scores = dot_nt(qv[rows, :], kvx[keys, 0:LW]) * scale
        kpos = s * ROWS + c * HALF - WMAX + iota((HALF, HALF + 2 * WMAX), 1)
        low = jnp.concatenate([lo_ref[rows, :]] * 3, axis=1)
        high = jnp.concatenate([hi_ref[rows, :]] * 3, axis=1)
        scores = jnp.where((kpos >= low) & (kpos <= high), scores, -1e30)
        peak = jnp.max(scores, axis=1, keepdims=True)
        weights = jnp.exp(scores - peak)
        weights = (weights / jnp.sum(weights, axis=1, keepdims=True)).astype(BF16)
        ctx[t, rows, :] = dot(weights, kvx[keys, LW : 2 * LW]).astype(BF16)
        sent1[c] = send_group(ctx, rows, c1s.at[c], c1r.at[c])

    for d in range(1, NX):
        wo_next[d - 1].wait_recv()
        give_wo(lax.rem(x_peer(NX - d) + NX, TP))
    w2_swap = []
    for k in range(1, TP):
        w2_first[k - 1].wait_recv()
        part = w2c.at[
            pl.ds(pl.multiple_of(lax.rem(t + TP - k, TP) * LW + core * 64, 64), 64)
        ]
        cp = remote(part, part, w2s.at[6 + k], w2r.at[6 + k], mate, t)
        cp.start()
        w2_swap.append(cp)

    for c in (1, 0):
        pass_on(ctx, slice(c * HALF, (c + 1) * HALF), c1s.at[c], c1r.at[c], sent1[c])
    for cp in wo_swap:
        cp.wait_recv()
    for cp in ld_w1:
        cp.wait()

    edges = {}
    for c in (1, 0):
        rows = slice(c * HALF, (c + 1) * HALF)
        attn = dot(whole(ctx, rows, sent1[c]), wof[...])
        resid = [
            (frame[q, rows, :].astype(F32) + attn[:, 256 * q : 256 * q + 256]).astype(BF16)
            for q in range(4)
        ]
        for q in range(4):
            res[2 * q, rows, :] = resid[q][:, 0:LW]
            res[2 * q + 1, rows, :] = resid[q][:, LW : 2 * LW]
        z2 = layer_norm([r.astype(F32) for r in resid], gain2)
        both = dot(z2, w1v[...])
        gated = (both[:, 0:LW] * jax.nn.sigmoid(both[:, LW : 2 * LW])).astype(BF16)
        glu[rows, :] = gated
        gluf[EDGE + c * HALF : EDGE + (c + 1) * HALF, :] = gated.astype(F32)
        if c == 1:
            cp = remote(glu.at[ROWS - EDGE : ROWS], rim.at[0], gs.at[0], gr.at[0], right, t)
        else:
            cp = remote(glu.at[0:EDGE], rim.at[1], gs.at[1], gr.at[1], left, t)
        cp.start()
        edges[c] = cp

    sent2 = {}
    for c in (1, 0):
        rows = slice(c * HALF, (c + 1) * HALF)
        edges[1 - c].wait_recv()
        if c == 1:
            gluf[EDGE + ROWS : 2 * EDGE + ROWS, :] = rim[1].astype(F32)
        else:
            gluf[0:EDGE, :] = rim[0].astype(F32)
        at = s * ROWS + c * HALF + iota((HALF, LW), 0)
        room_low = start_ref[rows, :] - at
        room_high = end_ref[rows, :] - at
        conv = jnp.zeros((HALF, LW), F32)
        for k in range(TAPS):
            first = EDGE + c * HALF + k - RIM
            valid = (room_low <= k - RIM) & (room_high > k - RIM)
            conv = conv + jnp.where(valid, gluf[first : first + HALF, :] * taps[k : k + 1, :], 0.0)
        shifted = conv * bn_scale[...] + bn_shift[...]
        act[t, rows, :] = (shifted * jax.nn.sigmoid(shifted)).astype(BF16)
        sent2[c] = send_group(act, rows, c2s.at[c], c2r.at[c])

    ld_w2.wait()
    for cp in w2_swap:
        cp.wait_recv()
    for c in (1, 0):
        pass_on(act, slice(c * HALF, (c + 1) * HALF), c2s.at[c], c2r.at[c], sent2[c])
    for c in (1, 0):
        rows = slice(c * HALF, (c + 1) * HALF)
        summed = dot(whole(act, rows, sent2[c]), w2c[...])
        out[rows, :] = (res[t, rows, :].astype(F32) + summed).astype(BF16)

    wait_all.wait_send()
    sends = swaps[0] + swaps[1] + halos + wo_first + wo_next + wo_swap + w2_first + w2_swap
    sends += sent1[0] + sent1[1] + sent2[0] + sent2[1] + [edges[0], edges[1]]
    for cp in sends:
        cp.wait_send()


def local(
    frames_in, stretch_map, rec_lengths, windows, ln1_gain, wqkv, wo, ln2_gain, w1,
    dw_kernel, bn_scale, bn_shift, w2,
):
    vmem = pl.BlockSpec(memory_space=pltpu.VMEM)
    smem = pl.BlockSpec(memory_space=pltpu.SMEM)
    hbm = pl.BlockSpec(memory_space=pl.ANY)
    dma = pltpu.SemaphoreType.DMA
    return pl.pallas_call(
        block_kernel,
        out_shape=jax.ShapeDtypeStruct((ROWS, LW), BF16),
        in_specs=[hbm, vmem, smem, smem, vmem, hbm, hbm, vmem, hbm, vmem, vmem, vmem, hbm],
        out_specs=vmem,
        scratch_shapes=[
            pltpu.VMEM((ROWS, 512), BF16),
            pltpu.VMEM((SEQ * MSG, 128), BF16),
            pltpu.VMEM((SEQ * MSG, 128), BF16),
            pltpu.VMEM((4, ROWS, 256), BF16),
            pltpu.VMEM((D, LW), BF16),
            pltpu.VMEM((D, 2 * LW), BF16),
            pltpu.VMEM((D, 2 * LW), BF16),
            pltpu.VMEM((D, D), BF16),
            pltpu.VMEM((D, LW), BF16),
            pltpu.VMEM((ROWS, LW), BF16),
            pltpu.VMEM((ROWS + 2 * WMAX, 2 * LW), BF16),
            pltpu.VMEM((TP, ROWS, LW), BF16),
            pltpu.VMEM((TP, ROWS, LW), BF16),
            pltpu.VMEM((TP, ROWS, LW), BF16),
            pltpu.VMEM((ROWS, LW), BF16),
            pltpu.VMEM((ROWS + 2 * EDGE, LW), F32),
            pltpu.VMEM((2, EDGE, LW), BF16),
            pltpu.VMEM((ROWS, LW), I32),
            pltpu.VMEM((ROWS, LW), I32),
            pltpu.VMEM((ROWS, LW), I32),
            pltpu.VMEM((ROWS, LW), I32),
            dma((8,)),
            dma,
            dma,
            dma,
            dma((2, 2)),
            dma((2, 2)),
            dma((2,)),
            dma((2,)),
            dma((14,)),
            dma((14,)),
            dma((14,)),
            dma((14,)),
            dma((2, 7)),
            dma((2, 7)),
            dma((2, 7)),
            dma((2, 7)),
            dma((2,)),
            dma((2,)),
        ],
        compiler_params=pltpu.CompilerParams(
            collective_id=0, has_side_effects=True, vmem_limit_bytes=48 << 20
        ),
        name="encoder_block",
    )(
        frames_in, stretch_map, rec_lengths, windows, ln1_gain.reshape(1, D), wqkv, wo,
        ln2_gain.reshape(1, D), w1, dw_kernel, bn_scale.reshape(1, LW),
        bn_shift.reshape(1, LW), w2,
    )


def solution(mesh):
    placed = (
        P("seq", None),
        P(),
        P(),
        P(),
        P(),
        P(None, None, "tp"),
        P("tp", None),
        P(),
        P(None, None, "tp"),
        P(None, "tp"),
        P("tp"),
        P("tp"),
        P("tp", None),
    )
    return jax.shard_map(
        local, mesh=mesh, in_specs=placed, out_specs=P("seq", "tp"), check_vma=False
    )
```

```python
import functools
import math

import jax
import jax.numpy as jnp
from jax import lax
from jax.experimental import pallas as pl
from jax.experimental.pallas import tpu as pltpu
from jax.sharding import PartitionSpec as P

MESH = pl.DeviceIdType.MESH
BF16 = jnp.bfloat16
F32 = jnp.float32
I32 = jnp.int32

SEQ = 64
TP = 8
NX = 4
ROWS = 256
HALF = 128
D = 1024
LW = 128
PIECE = 4
MSG = 16
WMAX = 128
TAPS = 9
RIM = 4
EDGE = 16


def dot(a, b):
    return jnp.dot(a, b, preferred_element_type=F32)


def dot_nt(a, b):
    return lax.dot_general(a, b, (((1,), (1,)), ((), ())), preferred_element_type=F32)


def iota(shape, dim):
    return lax.broadcasted_iota(I32, shape, dim)


def one_hot(mask):
    return jnp.where(mask, 1.0, 0.0).astype(BF16)


def layer_norm(blocks, gain_ref):
    width = blocks[0].shape[1]
    mean = sum(jnp.sum(b, axis=1, keepdims=True) for b in blocks) * (1.0 / D)
    centred = [b - mean for b in blocks]
    var = sum(jnp.sum(c * c, axis=1, keepdims=True) for c in centred) * (1.0 / D)
    inv = lax.rsqrt(var + 1e-05)
    normed = [
        (c * inv * gain_ref[:, i * width : (i + 1) * width]).astype(BF16)
        for i, c in enumerate(centred)
    ]
    return jnp.concatenate(normed, axis=1)


def block_kernel(
    frames, smap_hbm, lens_hbm, wins_hbm, gain1_hbm, wqkv, wo, gain2_hbm, w1, taps_hbm,
    bn_scale_hbm, bn_shift_hbm, w2,
    out,
    smap, lens, wins, gain1, gain2, taps, bn_scale, bn_shift,
    xin, sbuf, rbuf, frame, wq, wkv, w1v, wof, w2c, qv, kvx, ctx, act, res, glu, gluf, rim,
    lo_ref, hi_ref, start_ref, end_ref,
    ld, own_sem, a2a_s, a2a_r, xs, xr, hs, hr, wos, wor, w2s, w2r, c1s, c1r, c2s, c2r, gs, gr,
):
    s = lax.axis_index("seq")
    t = lax.axis_index("tp")
    z = t // NX
    x = lax.rem(t, NX)
    core = lax.rem(s, 2)
    mate = s + 1 - 2 * core
    left = lax.rem(s + SEQ - 1, SEQ)
    right = lax.rem(s + 1, SEQ)
    z_peer = lax.rem(t + NX, TP)

    def x_peer(d):
        return z * NX + lax.rem(x + d, NX)

    def remote(src, dst, send, recv, seq, tp):
        return pltpu.make_async_remote_copy(
            src_ref=src, dst_ref=dst, send_sem=send, recv_sem=recv,
            device_id=(seq, tp), device_id_type=MESH,
        )

    flight = []
    got = []

    def post(src, dst, send, recv, seq, tp):
        cp = remote(src, dst, send, recv, seq, tp)
        cp.start()
        flight.append(cp)
        return cp

    def land(cp):
        cp.wait_recv()
        got.append(id(cp))

    def drain():
        for cp in flight:
            if id(cp) not in got:
                cp.wait_recv()
            cp.wait_send()

    parity = lax.rem(x, 2)
    quarter = 2 * parity + x // 2
    loads = []

    def load(src, dst):
        cp = pltpu.make_async_copy(src, dst, ld.at[len(loads)])
        cp.start()
        loads.append(cp)
        return cp

    ld_frames = load(frames.at[:, pl.ds(pl.multiple_of(parity * 512, 512), 512)], xin)

    bar = pltpu.get_barrier_semaphore()

    def far_first(n):
        return lax.rem(s + SEQ // 2 + ((n + 1) // 2) * (1 - 2 * lax.rem(n, 2)), SEQ)

    def greet(n, carry):
        pl.semaphore_signal(bar, inc=1, device_id=(far_first(n), t), device_id_type=MESH)
        return carry

    for d in (4, 5, 3, 6, 2, 7, 1):
        pl.semaphore_signal(bar, inc=1, device_id=(s, lax.rem(t + d, TP)), device_id_type=MESH)
    lax.fori_loop(0, SEQ - 1, greet, 0)

    ld_wo = load(wo, wof.at[pl.ds(pl.multiple_of(t * LW, LW), LW)])
    ld_map = load(smap_hbm, smap)
    ld_rec = [load(lens_hbm, lens), load(wins_hbm, wins)]
    ld_qkv = [
        load(gain1_hbm, gain1),
        load(wqkv.at[1], wkv.at[:, 0:LW]),
        load(wqkv.at[2], wkv.at[:, LW : 2 * LW]),
        load(wqkv.at[0], wq),
    ]
    ld_conv = [
        load(taps_hbm, taps), load(bn_scale_hbm, bn_scale), load(bn_shift_hbm, bn_shift)
    ]
    ld_w1 = [load(gain2_hbm, gain2), load(w1.at[0], w1v.at[:, 0:LW]), load(w1.at[1], w1v.at[:, LW : 2 * LW])]
    ld_w2 = load(
        w2.at[:, pl.ds(pl.multiple_of(t * LW, LW), LW)],
        w2c.at[pl.ds(pl.multiple_of(t * LW, LW), LW)],
    )

    ld_frames.wait()
    o = iota((256, 256), 0)
    i = iota((256, 256), 1)
    pack = one_hot(i == 64 * ((o >> 2) & 3) + 4 * (o >> 4) + (o & 3))
    unpack = one_hot(o == 64 * ((i >> 2) & 3) + 4 * (i >> 4) + (i & 3))
    for g in range(4):
        stack = jnp.concatenate(
            [xin[64 * g : 64 * g + 64, 128 * c : 128 * c + 128] for c in range(4)], axis=0
        )
        sbuf[256 * g : 256 * g + 256, :] = dot(pack, stack).astype(BF16)

    pl.semaphore_wait(bar, SEQ - 1 + TP - 1)

    def rows16(index):
        return pl.ds(pl.multiple_of(index * MSG, MSG), MSG)

    def deal(n, carry):
        j = far_first(n)
        remote(sbuf.at[rows16(j)], rbuf.at[rows16(s)], a2a_s, a2a_r, j, t).start()
        return carry

    lax.fori_loop(0, SEQ - 1, deal, 0)
    own = pltpu.make_async_copy(sbuf.at[rows16(s)], rbuf.at[rows16(s)], own_sem)
    own.start()

    def wo_rows(tp, c):
        return wof.at[pl.ds(pl.multiple_of(tp * LW + c * 64, 64), 64)]

    def wo_block(tp, c, y):
        return wof.at[
            pl.ds(pl.multiple_of(tp * LW + c * 64, 64), 64), pl.ds(pl.multiple_of(y * LW, LW), LW)
        ]

    y = s // 8
    ld_wo.wait()
    part = wo_block(t, core, y)
    wo_cross = post(part, part, wos.at[3], wor.at[3], s, z_peer)
    wo_first = []
    for d in range(1, NX):
        part = wo_rows(t, core)
        wo_first.append(post(part, part, wos.at[d - 1], wor.at[d - 1], s, x_peer(d)))

    ld_map.wait()
    col = dot_nt(one_hot(iota((8, SEQ), 1) == s), smap[...].astype(F32).astype(BF16))
    spread = one_hot((iota((SEQ, 256), 1) >> 2) == iota((SEQ, 256), 0))
    place = dot(col.astype(BF16), spread) * 4.0 + (iota((8, 256), 1) & 3).astype(F32)
    order = one_hot(place[0:1, :] == o.astype(F32))

    for cp in ld_rec:
        cp.wait()
    pos = s * ROWS + iota((ROWS, LW), 0)
    start = jnp.zeros((ROWS, LW), I32)
    end = jnp.full((ROWS, LW), SEQ * ROWS, I32)
    reach = jnp.zeros((ROWS, LW), I32)
    total = jnp.int32(0)
    for k in range(8):
        before = total
        total = total + lens[k]
        start = jnp.where(pos >= total, total, start)
        end = jnp.where(pos < total, jnp.minimum(end, total), end)
        reach = jnp.where((pos >= before) & (pos < total), wins[k], reach)
    start_ref[...] = start
    end_ref[...] = end
    lo_ref[...] = jnp.maximum(start, pos - reach)
    hi_ref[...] = jnp.minimum(end - 1, pos + reach)

    own.wait()
    wait_all = remote(
        sbuf.at[0 : MSG * (SEQ - 1)], rbuf.at[0 : MSG * (SEQ - 1)], a2a_s, a2a_r, right, t
    )
    wait_all.wait_recv()
    parts = [dot(unpack, rbuf[256 * g : 256 * g + 256, :]).astype(BF16) for g in range(4)]
    dealt = jnp.concatenate(
        [
            jnp.concatenate([parts[g][64 * c : 64 * c + 64] for g in range(4)], axis=0)
            for c in range(4)
        ],
        axis=1,
    )
    ordered = dot(order, dealt).astype(BF16)
    frame[2 * parity] = ordered[:, 0:256]
    frame[2 * parity + 1] = ordered[:, 256:512]

    swaps = []
    for c in range(2):
        pair = []
        for n, d in enumerate((1, 3)):
            part = frame.at[quarter, c * HALF : (c + 1) * HALF]
            cp = post(part, part, xs.at[c, n], xr.at[c, n], s, x_peer(d))
            pair.append(cp)
        swaps.append(pair)

    land(wo_cross)
    wo_share = []
    for d in (4, 3, 5, 2, 6, 1, 7):
        part = wo_block(z_peer, core, y)
        k = 13 + d
        wo_share.append(post(part, part, wos.at[k], wor.at[k], lax.rem(s + 8 * d, SEQ), t))

    for cp in ld_qkv:
        cp.wait()
    halos = []
    for c in range(2):
        for cp in swaps[c]:
            land(cp)
        rows = slice(c * HALF, (c + 1) * HALF)
        z1 = layer_norm([frame[q, rows, :].astype(F32) for q in range(4)], gain1)
        kvx[WMAX + c * HALF : WMAX + (c + 1) * HALF, :] = dot(z1, wkv[...]).astype(BF16)
        src = kvx.at[WMAX + c * HALF : WMAX + (c + 1) * HALF]
        if c == 0:
            cp = post(src, kvx.at[WMAX + ROWS : 2 * WMAX + ROWS], hs.at[0], hr.at[0], left, t)
        else:
            cp = post(src, kvx.at[0:WMAX], hs.at[1], hr.at[1], right, t)
        halos.append(cp)
        qv[rows, :] = dot(z1, wq[...]).astype(BF16)

    for cp in wo_share:
        land(cp)
    wo_next = []
    for d in range(1, NX):
        cp = post(
            wo_rows(z_peer, core), wo_rows(z_peer, core), wos.at[3 + d], wor.at[3 + d], s, x_peer(d)
        )
        wo_next.append(cp)
    wo_swap = []

    def give_wo(tp):
        k = 7 + len(wo_swap)
        cp = post(wo_rows(tp, core), wo_rows(tp, core), wos.at[k], wor.at[k], mate, t)
        wo_swap.append(cp)

    give_wo(z_peer)
    for d in range(1, NX):
        land(wo_first[d - 1])
        give_wo(x_peer(NX - d))

    def send_group(buf, rows, send, recv):
        sent = []
        for k, peer in enumerate([z_peer, x_peer(1), x_peer(2), x_peer(3)]):
            cp = post(buf.at[t, rows], buf.at[t, rows], send.at[k], recv.at[k], s, peer)
            sent.append(cp)
        return sent

    def pass_on(buf, rows, send, recv, sent):
        land(sent[0])
        for d in range(1, NX):
            cp = post(
                buf.at[z_peer, rows], buf.at[z_peer, rows], send.at[3 + d], recv.at[3 + d],
                s, x_peer(d),
            )
            sent.append(cp)

    def whole(buf, rows, sent):
        for cp in sent[1:]:
            land(cp)
        return jnp.concatenate([buf[k, rows, :] for k in range(TP)], axis=1)

    EDGES = (slice(192, 256), slice(0, 64))
    PLACES = (slice(0, HALF), slice(HALF, ROWS))

    def natural(ref_rows, c):
        if c == 1:
            return ref_rows(slice(64, 192))
        return jnp.concatenate([ref_rows(e) for e in EDGES], axis=0)

    scale = 1.0 / math.sqrt(LW)

    def masked_scores(c, first, count):
        rows = slice(c * HALF, (c + 1) * HALF)
        scores = dot_nt(qv[rows, :], kvx[first : first + count, 0:LW]) * scale
        kpos = s * ROWS + first - WMAX + iota((HALF, count), 1)
        low = jnp.concatenate([lo_ref[rows, :]] * (count // LW), axis=1)
        high = jnp.concatenate([hi_ref[rows, :]] * (count // LW), axis=1)
        return jnp.where((kpos >= low) & (kpos <= high), scores, -1e30)

    def attend_own(c):
        scores = masked_scores(c, WMAX, ROWS)
        peak = jnp.max(scores, axis=1, keepdims=True)
        weights = jnp.exp(scores - peak)
        total = jnp.sum(weights, axis=1, keepdims=True)
        return peak, total, dot(weights.astype(BF16), kvx[WMAX : WMAX + ROWS, LW : 2 * LW])

    own_part = {c: attend_own(c) for c in (1, 0)}
    for c in (1, 0):
        first = 0 if c == 0 else WMAX + ROWS
        land(halos[1 - c])
        scores = masked_scores(c, first, WMAX)
        own_peak, own_total, own_sum = own_part[c]
        peak = jnp.maximum(own_peak, jnp.max(scores, axis=1, keepdims=True))
        weights = jnp.exp(scores - peak)
        fade = jnp.exp(own_peak - peak)
        total = own_total * fade + jnp.sum(weights, axis=1, keepdims=True)
        mixed = own_sum * fade + dot(weights.astype(BF16), kvx[first : first + WMAX, LW : 2 * LW])
        mixed = (mixed / total).astype(BF16)
        if c == 1:
            ctx[t, 0:64, :] = mixed[64:128]
            ctx[t, 192:256, :] = mixed[0:64]
        else:
            ctx[t, 64:192, :] = mixed
    sent1 = {}
    for c in (0, 1):
        sent1[c] = send_group(ctx, PLACES[c], c1s.at[c], c1r.at[c])

    for d in range(1, NX):
        land(wo_next[d - 1])
        give_wo(lax.rem(x_peer(NX - d) + NX, TP))
    for c in (0, 1):
        pass_on(ctx, PLACES[c], c1s.at[c], c1r.at[c], sent1[c])

    w2_first = []
    for k in (4, 5, 3, 6, 2, 7, 1):
        peer = lax.rem(t + k, TP)
        w2_first.append(
            post(
                w2.at[
                    pl.ds(pl.multiple_of(core * 64, 64), 64), pl.ds(pl.multiple_of(peer * LW, LW), LW)
                ],
                w2c.at[pl.ds(pl.multiple_of(t * LW + core * 64, 64), 64)],
                w2s.at[k - 1], w2r.at[k - 1], s, peer,
            )
        )

    for cp in wo_swap:
        land(cp)
    for cp in ld_w1:
        cp.wait()

    def conv_act(first, count):
        rows = slice(first, first + count)
        at = s * ROWS + first + iota((count, LW), 0)
        room_low = start_ref[rows, :] - at
        room_high = end_ref[rows, :] - at
        conv = jnp.zeros((count, LW), F32)
        for k in range(TAPS):
            begin = EDGE + first + k - RIM
            valid = (room_low <= k - RIM) & (room_high > k - RIM)
            conv = conv + jnp.where(valid, gluf[begin : begin + count, :] * taps[k : k + 1, :], 0.0)
        shifted = conv * bn_scale[...] + bn_shift[...]
        return (shifted * jax.nn.sigmoid(shifted)).astype(BF16)

    edges = []
    for c in (0, 1):
        attn = dot(whole(ctx, PLACES[c], sent1[c]), wof[...])
        resid = [
            (
                natural(lambda rows: frame[q, rows, :], c).astype(F32)
                + attn[:, 256 * q : 256 * q + 256]
            ).astype(BF16)
            for q in range(4)
        ]
        for q in range(4):
            res[2 * q, PLACES[c], :] = resid[q][:, 0:LW]
            res[2 * q + 1, PLACES[c], :] = resid[q][:, LW : 2 * LW]
        z2 = layer_norm([r.astype(F32) for r in resid], gain2)
        both = dot(z2, w1v[...])
        gated = (both[:, 0:LW] * jax.nn.sigmoid(both[:, LW : 2 * LW])).astype(BF16)
        if c == 0:
            glu[0] = gated[64 - EDGE : 64]
            glu[1] = gated[64 : 64 + EDGE]
            edges.append(post(glu.at[0], rim.at[0], gs.at[0], gr.at[0], right, t))
            edges.append(post(glu.at[1], rim.at[1], gs.at[1], gr.at[1], left, t))
            gluf[EDGE + 192 : EDGE + 256, :] = gated[0:64].astype(F32)
            gluf[EDGE : EDGE + 64, :] = gated[64:128].astype(F32)
        else:
            gluf[EDGE + 64 : EDGE + 192, :] = gated.astype(F32)

    sent2 = {}
    for cp in ld_conv:
        cp.wait()
    act[t, PLACES[1], :] = conv_act(64, HALF)
    sent2[1] = send_group(act, PLACES[1], c2s.at[1], c2r.at[1])
    land(edges[0])
    gluf[0:EDGE, :] = rim[0].astype(F32)
    land(edges[1])
    gluf[EDGE + ROWS : 2 * EDGE + ROWS, :] = rim[1].astype(F32)
    act[t, 0:64, :] = conv_act(192, 64)
    act[t, 64:128, :] = conv_act(0, 64)
    sent2[0] = send_group(act, PLACES[0], c2s.at[0], c2r.at[0])

    w2_swap = []
    for i, k in enumerate((4, 5, 3, 6, 2, 7, 1)):
        land(w2_first[i])
        part = w2c.at[pl.ds(pl.multiple_of(lax.rem(t + TP - k, TP) * LW + core * 64, 64), 64)]
        w2_swap.append(post(part, part, w2s.at[6 + k], w2r.at[6 + k], mate, t))
    for c in (1, 0):
        pass_on(act, PLACES[c], c2s.at[c], c2r.at[c], sent2[c])
    ld_w2.wait()
    for cp in w2_swap:
        land(cp)
    for c in (1, 0):
        summed = dot(whole(act, PLACES[c], sent2[c]), w2c[...])
        final = (res[t, PLACES[c], :].astype(F32) + summed).astype(BF16)
        if c == 1:
            out[64:192, :] = final
        else:
            out[192:256, :] = final[0:64]
            out[0:64, :] = final[64:128]

    wait_all.wait_send()
    drain()


def local(
    frames_in, stretch_map, rec_lengths, windows, ln1_gain, wqkv, wo, ln2_gain, w1,
    dw_kernel, bn_scale, bn_shift, w2,
):
    vmem = pl.BlockSpec(memory_space=pltpu.VMEM)
    hbm = pl.BlockSpec(memory_space=pl.ANY)
    dma = pltpu.SemaphoreType.DMA
    return pl.pallas_call(
        block_kernel,
        out_shape=jax.ShapeDtypeStruct((ROWS, LW), BF16),
        in_specs=[hbm] * 13,
        out_specs=vmem,
        scratch_shapes=[
            pltpu.VMEM((SEQ, SEQ), I32),
            pltpu.SMEM((8,), I32),
            pltpu.SMEM((8,), I32),
            pltpu.VMEM((1, D), F32),
            pltpu.VMEM((1, D), F32),
            pltpu.VMEM((TAPS, LW), F32),
            pltpu.VMEM((1, LW), F32),
            pltpu.VMEM((1, LW), F32),
            pltpu.VMEM((ROWS, 512), BF16),
            pltpu.VMEM((SEQ * MSG, 128), BF16),
            pltpu.VMEM((SEQ * MSG, 128), BF16),
            pltpu.VMEM((4, ROWS, 256), BF16),
            pltpu.VMEM((D, LW), BF16),
            pltpu.VMEM((D, 2 * LW), BF16),
            pltpu.VMEM((D, 2 * LW), BF16),
            pltpu.VMEM((D, D), BF16),
            pltpu.VMEM((D, LW), BF16),
            pltpu.VMEM((ROWS, LW), BF16),
            pltpu.VMEM((ROWS + 2 * WMAX, 2 * LW), BF16),
            pltpu.VMEM((TP, ROWS, LW), BF16),
            pltpu.VMEM((TP, ROWS, LW), BF16),
            pltpu.VMEM((TP, ROWS, LW), BF16),
            pltpu.VMEM((2, EDGE, LW), BF16),
            pltpu.VMEM((ROWS + 2 * EDGE, LW), F32),
            pltpu.VMEM((2, EDGE, LW), BF16),
            pltpu.VMEM((ROWS, LW), I32),
            pltpu.VMEM((ROWS, LW), I32),
            pltpu.VMEM((ROWS, LW), I32),
            pltpu.VMEM((ROWS, LW), I32),
            dma((16,)),
            dma,
            dma,
            dma,
            dma((2, 2)),
            dma((2, 2)),
            dma((2,)),
            dma((2,)),
            dma((21,)),
            dma((21,)),
            dma((14,)),
            dma((14,)),
            dma((2, 7)),
            dma((2, 7)),
            dma((2, 7)),
            dma((2, 7)),
            dma((2,)),
            dma((2,)),
        ],
        compiler_params=pltpu.CompilerParams(
            collective_id=0, has_side_effects=True, vmem_limit_bytes=60 << 20
        ),
        name="encoder_block",
    )(
        frames_in, stretch_map, rec_lengths, windows, ln1_gain.reshape(1, D), wqkv, wo,
        ln2_gain.reshape(1, D), w1, dw_kernel, bn_scale.reshape(1, LW),
        bn_shift.reshape(1, LW), w2,
    )


def solution(mesh):
    placed = (
        P("seq", None),
        P(),
        P(),
        P(),
        P(),
        P(None, None, "tp"),
        P("tp", None),
        P(),
        P(None, None, "tp"),
        P(None, "tp"),
        P("tp"),
        P("tp"),
        P("tp", None),
    )
    return jax.shard_map(
        local, mesh=mesh, in_specs=placed, out_specs=P("seq", "tp"), check_vma=False
    )
```

```python
import functools
import math

import jax
import jax.numpy as jnp
from jax import lax
from jax.experimental import pallas as pl
from jax.experimental.pallas import tpu as pltpu
from jax.sharding import PartitionSpec as P

MESH = pl.DeviceIdType.MESH
BF16 = jnp.bfloat16
F32 = jnp.float32
I32 = jnp.int32

SEQ = 64
TP = 8
NX = 4
ROWS = 256
HALF = 128
D = 1024
LW = 128
PIECE = 4
MSG = 8
WMAX = 128
TAPS = 9
RIM = 4
EDGE = 16


def dot(a, b):
    return jnp.dot(a, b, preferred_element_type=F32)


def dot_nt(a, b):
    return lax.dot_general(a, b, (((1,), (1,)), ((), ())), preferred_element_type=F32)


def iota(shape, dim):
    return lax.broadcasted_iota(I32, shape, dim)


def one_hot(mask):
    return jnp.where(mask, 1.0, 0.0).astype(BF16)


def layer_norm(blocks, gain_ref):
    width = blocks[0].shape[1]
    mean = sum(jnp.sum(b, axis=1, keepdims=True) for b in blocks) * (1.0 / D)
    centred = [b - mean for b in blocks]
    var = sum(jnp.sum(c * c, axis=1, keepdims=True) for c in centred) * (1.0 / D)
    inv = lax.rsqrt(var + 1e-05)
    normed = [
        (c * inv * gain_ref[:, i * width : (i + 1) * width]).astype(BF16)
        for i, c in enumerate(centred)
    ]
    return jnp.concatenate(normed, axis=1)


def block_kernel(
    frames, smap_hbm, lens_hbm, wins_hbm, gain1_hbm, wqkv, wo, gain2_hbm, w1, taps_hbm,
    bn_scale_hbm, bn_shift_hbm, w2,
    out,
    smap, lens, wins, gain1, gain2, taps, bn_scale, bn_shift,
    outv, xin, sbuf, rbuf, order, frame, wq, wkv, w1v, wof, w2c, qv, kvx, ctx, act, res, glu, gluf, rim,
    lo_ref, hi_ref, start_ref, end_ref,
    ld, out_sem, own_sem, a2a_s, a2a_r, xs, xr, hs, hr, wos, wor, w2s, w2r, c1s, c1r, c2s, c2r, gs, gr,
):
    s = lax.axis_index("seq")
    t = lax.axis_index("tp")
    z = t // NX
    x = lax.rem(t, NX)
    core = lax.rem(s, 2)
    mate = s + 1 - 2 * core
    left = lax.rem(s + SEQ - 1, SEQ)
    right = lax.rem(s + 1, SEQ)
    z_peer = lax.rem(t + NX, TP)

    def x_peer(d):
        return z * NX + lax.rem(x + d, NX)

    def remote(src, dst, send, recv, seq, tp):
        return pltpu.make_async_remote_copy(
            src_ref=src, dst_ref=dst, send_sem=send, recv_sem=recv,
            device_id=(seq, tp), device_id_type=MESH,
        )

    flight = []
    got = []

    def post(src, dst, send, recv, seq, tp):
        cp = remote(src, dst, send, recv, seq, tp)
        cp.start()
        flight.append(cp)
        return cp

    def land(cp):
        cp.wait_recv()
        got.append(id(cp))

    def drain():
        for cp in flight:
            if id(cp) not in got:
                cp.wait_recv()
            cp.wait_send()

    parity = lax.rem(x, 2)
    quarter = 2 * parity + x // 2
    loads = []

    def load(src, dst):
        cp = pltpu.make_async_copy(src, dst, ld.at[len(loads)])
        cp.start()
        loads.append(cp)
        return cp

    kept = 2 * parity + 1 - x // 2
    ld_frames = [
        load(frames.at[:, pl.ds(pl.multiple_of(q * 256, 256), 256)], xin.at[b])
        for b, q in enumerate((quarter, kept))
    ]

    bar = pltpu.get_barrier_semaphore()

    def far_first(n):
        return lax.rem(s + SEQ // 2 + ((n + 1) // 2) * (1 - 2 * lax.rem(n, 2)), SEQ)

    def greet(n, carry):
        pl.semaphore_signal(bar, inc=1, device_id=(far_first(n), t), device_id_type=MESH)
        return carry

    for d in (4, 5, 3, 6, 2, 7, 1):
        pl.semaphore_signal(bar, inc=1, device_id=(s, lax.rem(t + d, TP)), device_id_type=MESH)
    lax.fori_loop(0, SEQ - 1, greet, 0)

    ld_wo = load(wo, wof.at[pl.ds(pl.multiple_of(t * LW, LW), LW)])
    ld_map = load(smap_hbm, smap)
    ld_rec = [load(lens_hbm, lens), load(wins_hbm, wins)]
    ld_qkv = [
        load(gain1_hbm, gain1),
        load(wqkv.at[1], wkv.at[:, 0:LW]),
        load(wqkv.at[2], wkv.at[:, LW : 2 * LW]),
        load(wqkv.at[0], wq),
    ]
    ld_conv = [
        load(taps_hbm, taps), load(bn_scale_hbm, bn_scale), load(bn_shift_hbm, bn_shift)
    ]
    ld_w1 = [load(gain2_hbm, gain2), load(w1.at[0], w1v.at[:, 0:LW]), load(w1.at[1], w1v.at[:, LW : 2 * LW])]
    ld_w2 = load(
        w2.at[:, pl.ds(pl.multiple_of(t * LW, LW), LW)],
        w2c.at[pl.ds(pl.multiple_of(t * LW, LW), LW)],
    )

    for cp in ld_frames:
        cp.wait()
    o = iota((HALF, HALF), 0)
    pack = one_hot(iota((HALF, HALF), 1) == 64 * ((o >> 2) & 1) + 4 * (o >> 3) + (o & 3))
    for g in range(4):
        rows = slice(64 * g, 64 * g + 64)
        stack = jnp.concatenate(
            [
                jnp.concatenate([xin[b, rows, 0:128], xin[b, rows, 128:256]], axis=0)
                for b in range(2)
            ],
            axis=1,
        )
        packed = dot(pack, stack)
        for b in range(2):
            part = packed[:, 128 * b : 128 * b + 128].reshape(16, MSG, 128)
            sbuf[b, 16 * g : 16 * g + 16] = part.astype(BF16)

    pl.semaphore_wait(bar, SEQ - 1 + TP - 1)

    def wo_rows(tp, c):
        return wof.at[pl.ds(pl.multiple_of(tp * LW + c * 64, 64), 64)]

    def wo_block(tp, c, y):
        return wof.at[
            pl.ds(pl.multiple_of(tp * LW + c * 64, 64), 64), pl.ds(pl.multiple_of(y * LW, LW), LW)
        ]

    y = s // 8
    ld_wo.wait()
    part = wo_block(t, core, y)
    wo_cross = post(part, part, wos.at[3], wor.at[3], s, z_peer)
    wo_first = []
    for d in range(1, NX):
        part = wo_rows(t, core)
        wo_first.append(post(part, part, wos.at[d - 1], wor.at[d - 1], s, x_peer(d)))

    own = []
    deals = []
    for b in range(2):

        def deal(n, carry):
            j = far_first(n)
            remote(sbuf.at[b, j], rbuf.at[b, s], a2a_s.at[b], a2a_r.at[b], j, t).start()
            return carry

        lax.fori_loop(0, SEQ - 1, deal, 0)
        cp = pltpu.make_async_copy(sbuf.at[b, s], rbuf.at[b, s], own_sem.at[b])
        cp.start()
        own.append(cp)
        deals.append(
            remote(
                sbuf.at[b, 0 : SEQ - 1], rbuf.at[b, 0 : SEQ - 1], a2a_s.at[b], a2a_r.at[b], right, t
            )
        )

    ld_map.wait()
    col = dot_nt(one_hot(iota((8, SEQ), 1) == s), smap[...].astype(F32).astype(BF16))
    i = iota((8, SEQ * MSG), 1)
    spread = one_hot((iota((SEQ, SEQ * MSG), 1) >> 3) == iota((SEQ, SEQ * MSG), 0))
    place = dot(col.astype(BF16), spread) * 4.0 + (i & 3).astype(F32)
    o = iota((ROWS, SEQ * MSG), 0).astype(F32)
    for c in range(2):
        order[c] = one_hot(jnp.where(((i >> 2) & 1) == c, place, -1.0)[0:1, :] == o)

    for cp in ld_rec:
        cp.wait()
    pos = s * ROWS + iota((ROWS, LW), 0)
    start = jnp.zeros((ROWS, LW), I32)
    end = jnp.full((ROWS, LW), SEQ * ROWS, I32)
    reach = jnp.zeros((ROWS, LW), I32)
    total = jnp.int32(0)
    for k in range(8):
        before = total
        total = total + lens[k]
        start = jnp.where(pos >= total, total, start)
        end = jnp.where(pos < total, jnp.minimum(end, total), end)
        reach = jnp.where((pos >= before) & (pos < total), wins[k], reach)
    start_ref[...] = start
    end_ref[...] = end
    lo_ref[...] = jnp.maximum(start, pos - reach)
    hi_ref[...] = jnp.minimum(end - 1, pos + reach)

    def settle(b, q):
        own[b].wait()
        deals[b].wait_recv()
        dealt = rbuf[b].astype(F32).reshape(SEQ * MSG, 128).astype(BF16)
        for c in range(2):
            frame[q, :, 128 * c : 128 * c + 128] = dot(order[c], dealt).astype(BF16)

    land(wo_cross)
    part = wo_block(z_peer, core, y)
    wo_opposite = post(part, part, wos.at[4], wor.at[4], s, x_peer(2))

    settle(0, quarter)
    swaps = []
    for c in range(2):
        pair = []
        for n, d in enumerate((1, 3)):
            part = frame.at[quarter, c * HALF : (c + 1) * HALF]
            pair.append(post(part, part, xs.at[c, n], xr.at[c, n], s, x_peer(d)))
        swaps.append(pair)
    settle(1, kept)

    def share(tp, first):
        part = wo_block(tp, core, y)
        return [
            post(part, part, wos.at[first + d], wor.at[first + d], lax.rem(s + 8 * d, SEQ), t)
            for d in (4, 3, 5, 2, 6, 1, 7)
        ]

    wo_share = share(z_peer, 13)

    for cp in ld_qkv:
        cp.wait()
    halos = []
    for c in range(2):
        for cp in swaps[c]:
            land(cp)
        rows = slice(c * HALF, (c + 1) * HALF)
        z1 = layer_norm([frame[q, rows, :].astype(F32) for q in range(4)], gain1)
        kvx[WMAX + c * HALF : WMAX + (c + 1) * HALF, :] = dot(z1, wkv[...]).astype(BF16)
        src = kvx.at[WMAX + c * HALF : WMAX + (c + 1) * HALF]
        if c == 0:
            cp = post(src, kvx.at[WMAX + ROWS : 2 * WMAX + ROWS], hs.at[0], hr.at[0], left, t)
        else:
            cp = post(src, kvx.at[0:WMAX], hs.at[1], hr.at[1], right, t)
        halos.append(cp)
        qv[rows, :] = dot(z1, wq[...]).astype(BF16)

    for cp in wo_share:
        land(cp)
    wo_next = []
    for n, d in enumerate((1, 3)):
        part = wo_rows(z_peer, core)
        wo_next.append(post(part, part, wos.at[5 + n], wor.at[5 + n], s, x_peer(d)))
    wo_swap = []

    def give_wo(tp):
        k = 7 + len(wo_swap)
        cp = post(wo_rows(tp, core), wo_rows(tp, core), wos.at[k], wor.at[k], mate, t)
        wo_swap.append(cp)

    give_wo(z_peer)
    for d in range(1, NX):
        land(wo_first[d - 1])
        give_wo(x_peer(NX - d))

    x_peers = [x_peer(1), x_peer(2), x_peer(3)]

    def send_group(buf, rows, send, recv, peers, first):
        return [
            post(buf.at[t, rows], buf.at[t, rows], send.at[k], recv.at[k], s, peer)
            for k, peer in enumerate(peers, first)
        ]

    def pass_on(buf, rows, send, recv, sent):
        land(sent[0])
        for d in range(1, NX):
            cp = post(
                buf.at[z_peer, rows], buf.at[z_peer, rows], send.at[3 + d], recv.at[3 + d],
                s, x_peer(d),
            )
            sent.append(cp)

    def send_direct(buf, rows, send, recv):
        return [
            post(
                buf.at[t, rows], buf.at[t, rows], send.at[k], recv.at[k], s, lax.rem(t + d, TP)
            )
            for k, d in enumerate((4, 5, 3, 6, 2, 7, 1))
        ]

    def whole(buf, rows, sent):
        for cp in sent:
            if id(cp) not in got:
                land(cp)
        return jnp.concatenate([buf[k, rows, :] for k in range(TP)], axis=1)

    EDGES = (slice(192, 256), slice(0, 64))
    PLACES = (slice(0, HALF), slice(HALF, 192))
    BLOCKS = (slice(0, HALF), slice(HALF, ROWS))

    def natural(ref_rows, c):
        if c == 1:
            return ref_rows(slice(64, 192))
        return jnp.concatenate([ref_rows(e) for e in EDGES], axis=0)

    scale = 1.0 / math.sqrt(LW)

    def masked_scores(c, first, count):
        rows = slice(c * HALF, (c + 1) * HALF)
        scores = dot_nt(qv[rows, :], kvx[first : first + count, 0:LW]) * scale
        kpos = s * ROWS + first - WMAX + iota((HALF, count), 1)
        low = jnp.concatenate([lo_ref[rows, :]] * (count // LW), axis=1)
        high = jnp.concatenate([hi_ref[rows, :]] * (count // LW), axis=1)
        return jnp.where((kpos >= low) & (kpos <= high), scores, -1e30)

    def attend_own(c):
        scores = masked_scores(c, WMAX, ROWS)
        peak = jnp.max(scores, axis=1, keepdims=True)
        weights = jnp.exp(scores - peak)
        total = jnp.sum(weights, axis=1, keepdims=True)
        return peak, total, dot(weights.astype(BF16), kvx[WMAX : WMAX + ROWS, LW : 2 * LW])

    own_part = {c: attend_own(c) for c in (1, 0)}
    for c in (1, 0):
        first = 0 if c == 0 else WMAX + ROWS
        land(halos[1 - c])
        scores = masked_scores(c, first, WMAX)
        own_peak, own_total, own_sum = own_part[c]
        peak = jnp.maximum(own_peak, jnp.max(scores, axis=1, keepdims=True))
        weights = jnp.exp(scores - peak)
        fade = jnp.exp(own_peak - peak)
        total = own_total * fade + jnp.sum(weights, axis=1, keepdims=True)
        mixed = own_sum * fade + dot(weights.astype(BF16), kvx[first : first + WMAX, LW : 2 * LW])
        mixed = (mixed / total).astype(BF16)
        if c == 1:
            ctx[t, 0:64, :] = mixed[64:128]
            ctx[t, 192:256, :] = mixed[0:64]
        else:
            ctx[t, 64:192, :] = mixed
    sent1 = {}
    for c in (0, 1):
        sent1[c] = send_group(ctx, PLACES[c], c1s.at[c], c1r.at[c], [z_peer], 0)
    for c in (0, 1):
        sent1[c] += send_group(ctx, PLACES[c], c1s.at[c], c1r.at[c], x_peers, 1)
    straight = send_direct(ctx, slice(192, 256), c1s.at[2], c1r.at[2])

    z_opposite = lax.rem(x_peer(2) + NX, TP)
    land(wo_opposite)
    wo_share_opposite = share(z_opposite, 20)

    for n, d in enumerate((1, 3)):
        land(wo_next[n])
        give_wo(lax.rem(x_peer(NX - d) + NX, TP))
    for c in (0, 1):
        pass_on(ctx, PLACES[c], c1s.at[c], c1r.at[c], sent1[c])

    w2_first = []
    for k in (4, 5, 3, 6, 2, 7, 1):
        peer = lax.rem(t + k, TP)
        w2_first.append(
            post(
                w2.at[
                    pl.ds(pl.multiple_of(core * 64, 64), 64), pl.ds(pl.multiple_of(peer * LW, LW), LW)
                ],
                w2c.at[pl.ds(pl.multiple_of(t * LW + core * 64, 64), 64)],
                w2s.at[k - 1], w2r.at[k - 1], s, peer,
            )
        )

    for cp in wo_share_opposite:
        land(cp)
    give_wo(z_opposite)
    for cp in wo_swap:
        land(cp)
    for cp in ld_w1:
        cp.wait()

    def conv_act(first, count):
        rows = slice(first, first + count)
        at = s * ROWS + first + iota((count, LW), 0)
        room_low = start_ref[rows, :] - at
        room_high = end_ref[rows, :] - at
        conv = jnp.zeros((count, LW), F32)
        for k in range(TAPS):
            begin = EDGE + first + k - RIM
            valid = (room_low <= k - RIM) & (room_high > k - RIM)
            conv = conv + jnp.where(valid, gluf[begin : begin + count, :] * taps[k : k + 1, :], 0.0)
        shifted = conv * bn_scale[...] + bn_shift[...]
        return (shifted * jax.nn.sigmoid(shifted)).astype(BF16)

    edges = []
    for c in (0, 1):
        attn = dot(whole(ctx, BLOCKS[c], sent1[c] + straight * c), wof[...])
        resid = [
            (
                natural(lambda rows: frame[q, rows, :], c).astype(F32)
                + attn[:, 256 * q : 256 * q + 256]
            ).astype(BF16)
            for q in range(4)
        ]
        for q in range(4):
            for half in range(2):
                part = resid[q][:, half * LW : (half + 1) * LW]
                if c == 0:
                    res[2 * q + half, 192:256, :] = part[0:64]
                    res[2 * q + half, 0:64, :] = part[64:128]
                else:
                    res[2 * q + half, 64:192, :] = part
        z2 = layer_norm([r.astype(F32) for r in resid], gain2)
        both = dot(z2, w1v[...])
        gated = (both[:, 0:LW] * jax.nn.sigmoid(both[:, LW : 2 * LW])).astype(BF16)
        if c == 0:
            glu[0] = gated[64 - EDGE : 64]
            glu[1] = gated[64 : 64 + EDGE]
            edges.append(post(glu.at[0], rim.at[0], gs.at[0], gr.at[0], right, t))
            edges.append(post(glu.at[1], rim.at[1], gs.at[1], gr.at[1], left, t))
            gluf[EDGE + 192 : EDGE + 256, :] = gated[0:64].astype(F32)
            gluf[EDGE : EDGE + 64, :] = gated[64:128].astype(F32)
        else:
            gluf[EDGE + 64 : EDGE + 192, :] = gated.astype(F32)

    for cp in ld_conv:
        cp.wait()
    PIECES = ((0, 80), (80, 160), (160, 224))
    sent2 = []
    for n, (begin, stop) in enumerate(PIECES):
        act[t, begin:stop, :] = conv_act(EDGE + begin, stop - begin)
        sent2.append(
            send_group(act, slice(begin, stop), c2s.at[n], c2r.at[n], [z_peer], 0)
        )
    for n, (begin, stop) in enumerate(PIECES):
        sent2[n] += send_group(act, slice(begin, stop), c2s.at[n], c2r.at[n], x_peers, 1)
    land(edges[0])
    gluf[0:EDGE, :] = rim[0].astype(F32)
    land(edges[1])
    gluf[EDGE + ROWS : 2 * EDGE + ROWS, :] = rim[1].astype(F32)
    act[t, 224:240, :] = conv_act(ROWS - EDGE, EDGE)
    act[t, 240:256, :] = conv_act(0, EDGE)
    last = send_direct(act, slice(224, 256), c2s.at[3], c2r.at[3])

    w2_swap = []
    for n, k in enumerate((4, 5, 3, 6, 2, 7, 1)):
        land(w2_first[n])
        part = w2c.at[pl.ds(pl.multiple_of(lax.rem(t + TP - k, TP) * LW + core * 64, 64), 64)]
        w2_swap.append(post(part, part, w2s.at[6 + k], w2r.at[6 + k], mate, t))
    for n, (begin, stop) in enumerate(PIECES):
        pass_on(act, slice(begin, stop), c2s.at[n], c2r.at[n], sent2[n])
    ld_w2.wait()
    for cp in w2_swap:
        land(cp)

    def finish(first, count, begin, sent):
        summed = dot(whole(act, slice(begin, begin + count), sent), w2c[...])
        rows = slice(first, first + count)
        outv[rows, :] = (res[t, rows, :].astype(F32) + summed).astype(BF16)

    for n, (begin, stop) in enumerate(PIECES):
        finish(EDGE + begin, stop - begin, begin, sent2[n])
    finish(ROWS - EDGE, EDGE, 224, last)
    finish(0, EDGE, 240, last)
    cp = pltpu.make_async_copy(outv, out, out_sem)
    cp.start()
    cp.wait()

    for cp in deals:
        cp.wait_send()
    drain()


def local(
    frames_in, stretch_map, rec_lengths, windows, ln1_gain, wqkv, wo, ln2_gain, w1,
    dw_kernel, bn_scale, bn_shift, w2,
):
    hbm = pl.BlockSpec(memory_space=pl.ANY)
    dma = pltpu.SemaphoreType.DMA
    return pl.pallas_call(
        block_kernel,
        out_shape=jax.ShapeDtypeStruct((ROWS, LW), BF16),
        in_specs=[hbm] * 13,
        out_specs=hbm,
        scratch_shapes=[
            pltpu.VMEM((SEQ, SEQ), I32),
            pltpu.SMEM((8,), I32),
            pltpu.SMEM((8,), I32),
            pltpu.VMEM((1, D), F32),
            pltpu.VMEM((1, D), F32),
            pltpu.VMEM((TAPS, LW), F32),
            pltpu.VMEM((1, LW), F32),
            pltpu.VMEM((1, LW), F32),
            pltpu.VMEM((ROWS, LW), BF16),
            pltpu.VMEM((2, ROWS, 256), BF16),
            pltpu.VMEM((2, SEQ, MSG, 128), BF16),
            pltpu.VMEM((2, SEQ, MSG, 128), BF16),
            pltpu.VMEM((2, ROWS, SEQ * MSG), BF16),
            pltpu.VMEM((4, ROWS, 256), BF16),
            pltpu.VMEM((D, LW), BF16),
            pltpu.VMEM((D, 2 * LW), BF16),
            pltpu.VMEM((D, 2 * LW), BF16),
            pltpu.VMEM((D, D), BF16),
            pltpu.VMEM((D, LW), BF16),
            pltpu.VMEM((ROWS, LW), BF16),
            pltpu.VMEM((ROWS + 2 * WMAX, 2 * LW), BF16),
            pltpu.VMEM((TP, ROWS, LW), BF16),
            pltpu.VMEM((TP, ROWS, LW), BF16),
            pltpu.VMEM((TP, ROWS, LW), BF16),
            pltpu.VMEM((2, EDGE, LW), BF16),
            pltpu.VMEM((ROWS + 2 * EDGE, LW), F32),
            pltpu.VMEM((2, EDGE, LW), BF16),
            pltpu.VMEM((ROWS, LW), I32),
            pltpu.VMEM((ROWS, LW), I32),
            pltpu.VMEM((ROWS, LW), I32),
            pltpu.VMEM((ROWS, LW), I32),
            dma((17,)),
            dma,
            dma((2,)),
            dma((2,)),
            dma((2,)),
            dma((2, 2)),
            dma((2, 2)),
            dma((2,)),
            dma((2,)),
            dma((28,)),
            dma((28,)),
            dma((14,)),
            dma((14,)),
            dma((3, 7)),
            dma((3, 7)),
            dma((4, 7)),
            dma((4, 7)),
            dma((2,)),
            dma((2,)),
        ],
        compiler_params=pltpu.CompilerParams(
            collective_id=0, has_side_effects=True, vmem_limit_bytes=60 << 20
        ),
        name="encoder_block",
    )(
        frames_in, stretch_map, rec_lengths, windows, ln1_gain.reshape(1, D), wqkv, wo,
        ln2_gain.reshape(1, D), w1, dw_kernel, bn_scale.reshape(1, LW),
        bn_shift.reshape(1, LW), w2,
    )


def solution(mesh):
    placed = (
        P("seq", None),
        P(),
        P(),
        P(),
        P(),
        P(None, None, "tp"),
        P("tp", None),
        P(),
        P(None, None, "tp"),
        P(None, "tp"),
        P("tp"),
        P("tp"),
        P("tp", None),
    )
    return jax.shard_map(
        local, mesh=mesh, in_specs=placed, out_specs=P("seq", "tp"), check_vma=False
    )
```

```python
import functools
import math

import jax
import jax.numpy as jnp
from jax import lax
from jax.experimental import pallas as pl
from jax.experimental.pallas import tpu as pltpu
from jax.sharding import PartitionSpec as P

MESH = pl.DeviceIdType.MESH
BF16 = jnp.bfloat16
F32 = jnp.float32
I32 = jnp.int32

SEQ = 64
TP = 8
NX = 4
ROWS = 256
HALF = 128
D = 1024
LW = 128
PIECE = 4
MSG = 8
WMAX = 128
TAPS = 9
RIM = 4
EDGE = 16


def dot(a, b):
    return jnp.dot(a, b, preferred_element_type=F32)


def dot_nt(a, b):
    return lax.dot_general(a, b, (((1,), (1,)), ((), ())), preferred_element_type=F32)


def iota(shape, dim):
    return lax.broadcasted_iota(I32, shape, dim)


def one_hot(mask):
    return jnp.where(mask, 1.0, 0.0).astype(BF16)


def layer_norm(blocks, gain_ref):
    width = blocks[0].shape[1]
    mean = sum(jnp.sum(b, axis=1, keepdims=True) for b in blocks) * (1.0 / D)
    centred = [b - mean for b in blocks]
    var = sum(jnp.sum(c * c, axis=1, keepdims=True) for c in centred) * (1.0 / D)
    inv = lax.rsqrt(var + 1e-05)
    normed = [
        (c * inv * gain_ref[:, i * width : (i + 1) * width]).astype(BF16)
        for i, c in enumerate(centred)
    ]
    return jnp.concatenate(normed, axis=1)


def block_kernel(
    frames, smap_hbm, lens_hbm, wins_hbm, gain1_hbm, wqkv, wo, gain2_hbm, w1, taps_hbm,
    bn_scale_hbm, bn_shift_hbm, w2,
    out,
    smap, lens, wins, gain1, gain2, taps, bn_scale, bn_shift,
    outv, xin, sbuf, rbuf, order, frame, wq, wkv, w1v, wof, w2c, qv, kvx, ctx, act, res, glu, gluf, rim,
    lo_ref, hi_ref, start_ref, end_ref,
    ld, out_sem, own_sem, a2a_s, a2a_r, xs, xr, hs, hr, wos, wor, w2s, w2r, c1s, c1r, c2s, c2r, gs, gr,
):
    s = lax.axis_index("seq")
    t = lax.axis_index("tp")
    z = t // NX
    x = lax.rem(t, NX)
    core = lax.rem(s, 2)
    mate = s + 1 - 2 * core
    left = lax.rem(s + SEQ - 1, SEQ)
    right = lax.rem(s + 1, SEQ)
    z_peer = lax.rem(t + NX, TP)

    def x_peer(d):
        return z * NX + lax.rem(x + d, NX)

    def remote(src, dst, send, recv, seq, tp):
        return pltpu.make_async_remote_copy(
            src_ref=src, dst_ref=dst, send_sem=send, recv_sem=recv,
            device_id=(seq, tp), device_id_type=MESH,
        )

    flight = []
    got = []

    def post(src, dst, send, recv, seq, tp):
        cp = remote(src, dst, send, recv, seq, tp)
        cp.start()
        flight.append(cp)
        return cp

    def land(cp):
        cp.wait_recv()
        got.append(id(cp))

    def drain():
        for cp in flight:
            if id(cp) not in got:
                cp.wait_recv()
            cp.wait_send()

    parity = lax.rem(x, 2)
    quarter = 2 * parity + x // 2
    loads = []

    def load(src, dst):
        cp = pltpu.make_async_copy(src, dst, ld.at[len(loads)])
        cp.start()
        loads.append(cp)
        return cp

    kept = 2 * parity + 1 - x // 2
    ld_frames = [
        load(frames.at[:, pl.ds(pl.multiple_of(q * 256, 256), 256)], xin.at[b])
        for b, q in enumerate((quarter, kept))
    ]

    bar = pltpu.get_barrier_semaphore()

    def far_first(n):
        return lax.rem(s + SEQ // 2 + ((n + 1) // 2) * (1 - 2 * lax.rem(n, 2)), SEQ)

    def greet(n, carry):
        pl.semaphore_signal(bar, inc=1, device_id=(far_first(n), t), device_id_type=MESH)
        return carry

    for d in (4, 5, 3, 6, 2, 7, 1):
        pl.semaphore_signal(bar, inc=1, device_id=(s, lax.rem(t + d, TP)), device_id_type=MESH)
    lax.fori_loop(0, SEQ - 1, greet, 0)

    ld_wo = load(wo, wof.at[pl.ds(pl.multiple_of(t * LW, LW), LW)])
    ld_map = load(smap_hbm, smap)
    ld_rec = [load(lens_hbm, lens), load(wins_hbm, wins)]
    ld_qkv = [
        load(gain1_hbm, gain1),
        load(wqkv.at[1], wkv.at[:, 0:LW]),
        load(wqkv.at[2], wkv.at[:, LW : 2 * LW]),
        load(wqkv.at[0], wq),
    ]
    ld_conv = [
        load(taps_hbm, taps), load(bn_scale_hbm, bn_scale), load(bn_shift_hbm, bn_shift)
    ]
    ld_w1 = [load(gain2_hbm, gain2), load(w1.at[0], w1v.at[:, 0:LW]), load(w1.at[1], w1v.at[:, LW : 2 * LW])]
    ld_w2 = load(
        w2.at[:, pl.ds(pl.multiple_of(t * LW, LW), LW)],
        w2c.at[pl.ds(pl.multiple_of(t * LW, LW), LW)],
    )

    for cp in ld_frames:
        cp.wait()
    o = iota((HALF, HALF), 0)
    pack = one_hot(iota((HALF, HALF), 1) == 64 * ((o >> 2) & 1) + 4 * (o >> 3) + (o & 3))
    for g in range(4):
        rows = slice(64 * g, 64 * g + 64)
        stack = jnp.concatenate(
            [
                jnp.concatenate([xin[b, rows, 0:128], xin[b, rows, 128:256]], axis=0)
                for b in range(2)
            ],
            axis=1,
        )
        packed = dot(pack, stack)
        for b in range(2):
            part = packed[:, 128 * b : 128 * b + 128].reshape(16, MSG, 128)
            sbuf[b, 16 * g : 16 * g + 16] = part.astype(BF16)

    pl.semaphore_wait(bar, SEQ - 1 + TP - 1)

    def wo_rows(tp, c):
        return wof.at[pl.ds(pl.multiple_of(tp * LW + c * 64, 64), 64)]

    def wo_block(tp, c, y):
        return wof.at[
            pl.ds(pl.multiple_of(tp * LW + c * 64, 64), 64), pl.ds(pl.multiple_of(y * LW, LW), LW)
        ]

    y = s // 8
    ld_wo.wait()
    part = wo_block(t, core, y)
    wo_cross = post(part, part, wos.at[3], wor.at[3], s, z_peer)
    wo_first = []
    for d in range(1, NX):
        part = wo_rows(t, core)
        wo_first.append(post(part, part, wos.at[d - 1], wor.at[d - 1], s, x_peer(d)))

    own = []
    deals = []
    for b in range(2):

        def deal(n, carry):
            j = far_first(n)
            remote(sbuf.at[b, j], rbuf.at[b, s], a2a_s.at[b], a2a_r.at[b], j, t).start()
            return carry

        lax.fori_loop(0, SEQ - 1, deal, 0)
        cp = pltpu.make_async_copy(sbuf.at[b, s], rbuf.at[b, s], own_sem.at[b])
        cp.start()
        own.append(cp)
        deals.append(
            remote(
                sbuf.at[b, 0 : SEQ - 1], rbuf.at[b, 0 : SEQ - 1], a2a_s.at[b], a2a_r.at[b], right, t
            )
        )

    ld_map.wait()
    col = dot_nt(one_hot(iota((8, SEQ), 1) == s), smap[...].astype(F32).astype(BF16))
    i = iota((8, SEQ * MSG), 1)
    spread = one_hot((iota((SEQ, SEQ * MSG), 1) >> 3) == iota((SEQ, SEQ * MSG), 0))
    place = dot(col.astype(BF16), spread) * 4.0 + (i & 3).astype(F32)
    o = iota((ROWS, SEQ * MSG), 0).astype(F32)
    for c in range(2):
        order[c] = one_hot(jnp.where(((i >> 2) & 1) == c, place, -1.0)[0:1, :] == o)

    for cp in ld_rec:
        cp.wait()
    pos = s * ROWS + iota((ROWS, LW), 0)
    start = jnp.zeros((ROWS, LW), I32)
    end = jnp.full((ROWS, LW), SEQ * ROWS, I32)
    reach = jnp.zeros((ROWS, LW), I32)
    total = jnp.int32(0)
    for k in range(8):
        before = total
        total = total + lens[k]
        start = jnp.where(pos >= total, total, start)
        end = jnp.where(pos < total, jnp.minimum(end, total), end)
        reach = jnp.where((pos >= before) & (pos < total), wins[k], reach)
    start_ref[...] = start
    end_ref[...] = end
    lo_ref[...] = jnp.maximum(start, pos - reach)
    hi_ref[...] = jnp.minimum(end - 1, pos + reach)

    def settle(b, q):
        own[b].wait()
        deals[b].wait_recv()
        dealt = rbuf[b].astype(F32).reshape(SEQ * MSG, 128).astype(BF16)
        for c in range(2):
            frame[q, :, 128 * c : 128 * c + 128] = dot(order[c], dealt).astype(BF16)

    land(wo_cross)
    part = wo_block(z_peer, core, y)
    wo_opposite = post(part, part, wos.at[4], wor.at[4], s, x_peer(2))

    settle(0, quarter)
    def half_rows(c, first=0, count=HALF):
        return pl.ds(pl.multiple_of(c * HALF + first, 64), count)

    FAR_NEAR = ((0, core, jnp.where(core == 0, left, right)), (1, 1 - core, mate))
    swaps = []
    for k, c, _ in FAR_NEAR:
        part = frame.at[quarter, half_rows(c)]
        swaps.append(
            [post(part, part, xs.at[k, n], xr.at[k, n], s, x_peer(d)) for n, d in enumerate((1, 3))]
        )
    settle(1, kept)

    def share(tp, first):
        part = wo_block(tp, core, y)
        return [
            post(part, part, wos.at[first + d], wor.at[first + d], lax.rem(s + 8 * d, SEQ), t)
            for d in (4, 3, 5, 2, 6, 1, 7)
        ]

    wo_share = share(z_peer, 13)

    def group_peer(k):
        return lax.rem(x_peer(k % NX) + k // NX * NX, TP)

    w2_first = {}

    def give_w2(steps):
        for k in steps:
            peer = group_peer(k)
            cols = pl.ds(pl.multiple_of(peer * LW, LW), LW)
            w2_first[k] = post(
                w2.at[pl.ds(pl.multiple_of(core * 64, 64), 64), cols],
                w2c.at[pl.ds(pl.multiple_of(t * LW + core * 64, 64), 64)],
                w2s.at[k - 1], w2r.at[k - 1], s, peer,
            )

    give_w2(range(NX, TP))

    for cp in ld_qkv:
        cp.wait()
    halos = []
    normed = []
    for k, c, peer in FAR_NEAR:
        for cp in swaps[k]:
            land(cp)
        z1 = layer_norm([frame[q, half_rows(c), :].astype(F32) for q in range(4)], gain1)
        normed.append(z1)
        here = half_rows(c, WMAX)
        kvx[here, :] = dot(z1, wkv[...]).astype(BF16)
        there = half_rows(3 * (1 - c))
        halos.append(post(kvx.at[here], kvx.at[there], hs.at[k], hr.at[k], peer, t))
    for k, c, _ in FAR_NEAR:
        qv[half_rows(c), :] = dot(normed[k], wq[...]).astype(BF16)

    for cp in wo_share:
        land(cp)
    wo_next = []
    for n, d in enumerate((1, 3)):
        part = wo_rows(z_peer, core)
        wo_next.append(post(part, part, wos.at[5 + n], wor.at[5 + n], s, x_peer(d)))
    wo_swap = []

    def give_wo(tp):
        k = 7 + len(wo_swap)
        cp = post(wo_rows(tp, core), wo_rows(tp, core), wos.at[k], wor.at[k], mate, t)
        wo_swap.append(cp)

    give_wo(z_peer)
    for d in range(1, NX):
        land(wo_first[d - 1])
        give_wo(x_peer(NX - d))

    x_peers = [x_peer(1), x_peer(2), x_peer(3)]

    def send_group(buf, rows, send, recv, peers, first):
        return [
            post(buf.at[t, rows], buf.at[t, rows], send.at[k], recv.at[k], s, peer)
            for k, peer in enumerate(peers, first)
        ]

    def pass_on(buf, rows, send, recv, sent):
        land(sent[0])
        for d in range(1, NX):
            cp = post(
                buf.at[z_peer, rows], buf.at[z_peer, rows], send.at[3 + d], recv.at[3 + d],
                s, x_peer(d),
            )
            sent.append(cp)

    def send_direct(buf, rows, send, recv):
        return [
            post(
                buf.at[t, rows], buf.at[t, rows], send.at[k], recv.at[k], s, lax.rem(t + d, TP)
            )
            for k, d in enumerate((4, 5, 3, 6, 2, 7, 1))
        ]

    def whole(buf, rows, sent):
        for cp in sent:
            if id(cp) not in got:
                land(cp)
        return jnp.concatenate([buf[k, rows, :] for k in range(TP)], axis=1)

    EDGES = (slice(192, 256), slice(0, 64))
    PLACES = (slice(0, HALF), slice(HALF, ROWS))
    BLOCKS = (slice(0, HALF), slice(HALF, ROWS))

    def natural(ref_rows, c):
        if c == 1:
            return ref_rows(slice(64, 192))
        return jnp.concatenate([ref_rows(e) for e in EDGES], axis=0)

    scale = 1.0 / math.sqrt(LW)

    def masked_scores(c, first, count):
        rows = half_rows(c)
        scores = dot_nt(qv[rows, :], kvx[pl.ds(first, count), 0:LW]) * scale
        kpos = s * ROWS + first - WMAX + iota((HALF, count), 1)
        low = jnp.concatenate([lo_ref[rows, :]] * (count // LW), axis=1)
        high = jnp.concatenate([hi_ref[rows, :]] * (count // LW), axis=1)
        return jnp.where((kpos >= low) & (kpos <= high), scores, -1e30)

    def attend_own(c):
        scores = masked_scores(c, WMAX, ROWS)
        peak = jnp.max(scores, axis=1, keepdims=True)
        weights = jnp.exp(scores - peak)
        total = jnp.sum(weights, axis=1, keepdims=True)
        return peak, total, dot(weights.astype(BF16), kvx[WMAX : WMAX + ROWS, LW : 2 * LW])

    own_part = [attend_own(c) for _, c, _ in FAR_NEAR]
    for k in (1, 0):
        c = FAR_NEAR[k][1]
        first = pl.multiple_of(c * (WMAX + ROWS), HALF)
        land(halos[k])
        scores = masked_scores(c, first, WMAX)
        own_peak, own_total, own_sum = own_part[k]
        peak = jnp.maximum(own_peak, jnp.max(scores, axis=1, keepdims=True))
        weights = jnp.exp(scores - peak)
        fade = jnp.exp(own_peak - peak)
        total = own_total * fade + jnp.sum(weights, axis=1, keepdims=True)
        mixed = own_sum * fade + dot(weights.astype(BF16), kvx[pl.ds(first, WMAX), LW : 2 * LW])
        mixed = (mixed / total).astype(BF16)
        ctx[t, half_rows(c, 64, 64), :] = mixed[0:64]
        ctx[t, half_rows(1 - c, 0, 64), :] = mixed[64:128]
    sent1 = {}
    for c in (0, 1):
        sent1[c] = send_group(ctx, PLACES[c], c1s.at[c], c1r.at[c], [z_peer], 0)
    for c in (0, 1):
        sent1[c] += send_group(ctx, PLACES[c], c1s.at[c], c1r.at[c], x_peers, 1)

    z_opposite = lax.rem(x_peer(2) + NX, TP)
    land(wo_opposite)
    wo_share_opposite = share(z_opposite, 20)

    for n, d in enumerate((1, 3)):
        land(wo_next[n])
        give_wo(lax.rem(x_peer(NX - d) + NX, TP))
    for c in (0, 1):
        pass_on(ctx, PLACES[c], c1s.at[c], c1r.at[c], sent1[c])

    give_w2(range(1, NX))

    for cp in wo_share_opposite:
        land(cp)
    give_wo(z_opposite)
    for cp in wo_swap:
        land(cp)
    for cp in ld_w1:
        cp.wait()

    def conv_act(first, count):
        rows = slice(first, first + count)
        at = s * ROWS + first + iota((count, LW), 0)
        room_low = start_ref[rows, :] - at
        room_high = end_ref[rows, :] - at
        conv = jnp.zeros((count, LW), F32)
        for k in range(TAPS):
            begin = EDGE + first + k - RIM
            valid = (room_low <= k - RIM) & (room_high > k - RIM)
            conv = conv + jnp.where(valid, gluf[begin : begin + count, :] * taps[k : k + 1, :], 0.0)
        shifted = conv * bn_scale[...] + bn_shift[...]
        return (shifted * jax.nn.sigmoid(shifted)).astype(BF16)

    edges = []
    for c in (0, 1):
        attn = dot(whole(ctx, BLOCKS[c], sent1[c]), wof[...])
        resid = [
            (
                natural(lambda rows: frame[q, rows, :], c).astype(F32)
                + attn[:, 256 * q : 256 * q + 256]
            ).astype(BF16)
            for q in range(4)
        ]
        for q in range(4):
            for half in range(2):
                part = resid[q][:, half * LW : (half + 1) * LW]
                if c == 0:
                    res[2 * q + half, 192:256, :] = part[0:64]
                    res[2 * q + half, 0:64, :] = part[64:128]
                else:
                    res[2 * q + half, 64:192, :] = part
        z2 = layer_norm([r.astype(F32) for r in resid], gain2)
        both = dot(z2, w1v[...])
        gated = (both[:, 0:LW] * jax.nn.sigmoid(both[:, LW : 2 * LW])).astype(BF16)
        if c == 0:
            glu[0] = gated[64 - EDGE : 64]
            glu[1] = gated[64 : 64 + EDGE]
            edges.append(post(glu.at[0], rim.at[0], gs.at[0], gr.at[0], right, t))
            edges.append(post(glu.at[1], rim.at[1], gs.at[1], gr.at[1], left, t))
            gluf[EDGE + 192 : EDGE + 256, :] = gated[0:64].astype(F32)
            gluf[EDGE : EDGE + 64, :] = gated[64:128].astype(F32)
        else:
            gluf[EDGE + 64 : EDGE + 192, :] = gated.astype(F32)

    for cp in ld_conv:
        cp.wait()
    PIECES = ((0, 80), (80, 160), (160, 224))
    sent2 = []
    for n, (begin, stop) in enumerate(PIECES):
        act[t, begin:stop, :] = conv_act(EDGE + begin, stop - begin)
        sent2.append(
            send_group(act, slice(begin, stop), c2s.at[n], c2r.at[n], [z_peer], 0)
        )
    for n, (begin, stop) in enumerate(PIECES):
        sent2[n] += send_group(act, slice(begin, stop), c2s.at[n], c2r.at[n], x_peers, 1)
    land(edges[0])
    gluf[0:EDGE, :] = rim[0].astype(F32)
    land(edges[1])
    gluf[EDGE + ROWS : 2 * EDGE + ROWS, :] = rim[1].astype(F32)
    act[t, 224:240, :] = conv_act(ROWS - EDGE, EDGE)
    act[t, 240:256, :] = conv_act(0, EDGE)
    last = send_direct(act, slice(224, 256), c2s.at[3], c2r.at[3])

    w2_swap = []
    for k in (4, 5, 6, 7, 1, 2, 3):
        land(w2_first[k])
        source = group_peer(k // NX * NX + (NX - k) % NX)
        part = w2c.at[pl.ds(pl.multiple_of(source * LW + core * 64, 64), 64)]
        w2_swap.append(post(part, part, w2s.at[6 + k], w2r.at[6 + k], mate, t))
    for n, (begin, stop) in enumerate(PIECES):
        pass_on(act, slice(begin, stop), c2s.at[n], c2r.at[n], sent2[n])
    ld_w2.wait()
    for cp in w2_swap:
        land(cp)

    def finish(first, count, begin, sent):
        summed = dot(whole(act, slice(begin, begin + count), sent), w2c[...])
        rows = slice(first, first + count)
        outv[rows, :] = (res[t, rows, :].astype(F32) + summed).astype(BF16)

    for n, (begin, stop) in enumerate(PIECES):
        finish(EDGE + begin, stop - begin, begin, sent2[n])
    finish(ROWS - EDGE, EDGE, 224, last)
    finish(0, EDGE, 240, last)
    cp = pltpu.make_async_copy(outv, out, out_sem)
    cp.start()
    cp.wait()

    for cp in deals:
        cp.wait_send()
    drain()


def local(
    frames_in, stretch_map, rec_lengths, windows, ln1_gain, wqkv, wo, ln2_gain, w1,
    dw_kernel, bn_scale, bn_shift, w2,
):
    hbm = pl.BlockSpec(memory_space=pl.ANY)
    dma = pltpu.SemaphoreType.DMA
    return pl.pallas_call(
        block_kernel,
        out_shape=jax.ShapeDtypeStruct((ROWS, LW), BF16),
        in_specs=[hbm] * 13,
        out_specs=hbm,
        scratch_shapes=[
            pltpu.VMEM((SEQ, SEQ), I32),
            pltpu.SMEM((8,), I32),
            pltpu.SMEM((8,), I32),
            pltpu.VMEM((1, D), F32),
            pltpu.VMEM((1, D), F32),
            pltpu.VMEM((TAPS, LW), F32),
            pltpu.VMEM((1, LW), F32),
            pltpu.VMEM((1, LW), F32),
            pltpu.VMEM((ROWS, LW), BF16),
            pltpu.VMEM((2, ROWS, 256), BF16),
            pltpu.VMEM((2, SEQ, MSG, 128), BF16),
            pltpu.VMEM((2, SEQ, MSG, 128), BF16),
            pltpu.VMEM((2, ROWS, SEQ * MSG), BF16),
            pltpu.VMEM((4, ROWS, 256), BF16),
            pltpu.VMEM((D, LW), BF16),
            pltpu.VMEM((D, 2 * LW), BF16),
            pltpu.VMEM((D, 2 * LW), BF16),
            pltpu.VMEM((D, D), BF16),
            pltpu.VMEM((D, LW), BF16),
            pltpu.VMEM((ROWS, LW), BF16),
            pltpu.VMEM((ROWS + 2 * WMAX, 2 * LW), BF16),
            pltpu.VMEM((TP, ROWS, LW), BF16),
            pltpu.VMEM((TP, ROWS, LW), BF16),
            pltpu.VMEM((TP, ROWS, LW), BF16),
            pltpu.VMEM((2, EDGE, LW), BF16),
            pltpu.VMEM((ROWS + 2 * EDGE, LW), F32),
            pltpu.VMEM((2, EDGE, LW), BF16),
            pltpu.VMEM((ROWS, LW), I32),
            pltpu.VMEM((ROWS, LW), I32),
            pltpu.VMEM((ROWS, LW), I32),
            pltpu.VMEM((ROWS, LW), I32),
            dma((17,)),
            dma,
            dma((2,)),
            dma((2,)),
            dma((2,)),
            dma((2, 2)),
            dma((2, 2)),
            dma((2,)),
            dma((2,)),
            dma((28,)),
            dma((28,)),
            dma((14,)),
            dma((14,)),
            dma((3, 7)),
            dma((3, 7)),
            dma((4, 7)),
            dma((4, 7)),
            dma((2,)),
            dma((2,)),
        ],
        compiler_params=pltpu.CompilerParams(
            collective_id=0, has_side_effects=True, vmem_limit_bytes=60 << 20
        ),
        name="encoder_block",
    )(
        frames_in, stretch_map, rec_lengths, windows, ln1_gain.reshape(1, D), wqkv, wo,
        ln2_gain.reshape(1, D), w1, dw_kernel, bn_scale.reshape(1, LW),
        bn_shift.reshape(1, LW), w2,
    )


def solution(mesh):
    placed = (
        P("seq", None),
        P(),
        P(),
        P(),
        P(),
        P(None, None, "tp"),
        P("tp", None),
        P(),
        P(None, None, "tp"),
        P(None, "tp"),
        P("tp"),
        P("tp"),
        P("tp", None),
    )
    return jax.shard_map(
        local, mesh=mesh, in_specs=placed, out_specs=P("seq", "tp"), check_vma=False
    )
```

```python
import functools
import math

import jax
import jax.numpy as jnp
from jax import lax
from jax.experimental import pallas as pl
from jax.experimental.pallas import tpu as pltpu
from jax.sharding import PartitionSpec as P

MESH = pl.DeviceIdType.MESH
BF16 = jnp.bfloat16
F32 = jnp.float32
I32 = jnp.int32

SEQ = 64
TP = 8
NX = 4
ROWS = 256
HALF = 128
D = 1024
LW = 128
PIECE = 4
MSG = 8
WMAX = 128
TAPS = 9
RIM = 4
EDGE = 16


def dot(a, b):
    return jnp.dot(a, b, preferred_element_type=F32)


def dot_nt(a, b):
    return lax.dot_general(a, b, (((1,), (1,)), ((), ())), preferred_element_type=F32)


def iota(shape, dim):
    return lax.broadcasted_iota(I32, shape, dim)


def one_hot(mask):
    return jnp.where(mask, 1.0, 0.0).astype(BF16)


def layer_norm(blocks, gain_ref):
    width = blocks[0].shape[1]
    mean = sum(jnp.sum(b, axis=1, keepdims=True) for b in blocks) * (1.0 / D)
    centred = [b - mean for b in blocks]
    var = sum(jnp.sum(c * c, axis=1, keepdims=True) for c in centred) * (1.0 / D)
    inv = lax.rsqrt(var + 1e-05)
    normed = [
        (c * inv * gain_ref[:, i * width : (i + 1) * width]).astype(BF16)
        for i, c in enumerate(centred)
    ]
    return jnp.concatenate(normed, axis=1)


def block_kernel(
    frames, smap_hbm, lens_hbm, wins_hbm, gain1_hbm, wqkv, wo, gain2_hbm, w1, taps_hbm,
    bn_scale_hbm, bn_shift_hbm, w2,
    out,
    smap, lens, wins, gain1, gain2, taps, bn_scale, bn_shift,
    outv, xin, sbuf, rbuf, order, frame, wq, wkv, w1v, wof, w2c, qv, kvx, ctx, act, res, glu, gluf, rim,
    lo_ref, hi_ref, start_ref, end_ref,
    ld, out_sem, own_sem, a2a_s, a2a_r, xs, xr, hs, hr, wos, wor, w2s, w2r, c1s, c1r, c2s, c2r, gs, gr,
):
    s = lax.axis_index("seq")
    t = lax.axis_index("tp")
    z = t // NX
    x = lax.rem(t, NX)
    core = lax.rem(s, 2)
    mate = s + 1 - 2 * core
    left = lax.rem(s + SEQ - 1, SEQ)
    right = lax.rem(s + 1, SEQ)
    z_peer = lax.rem(t + NX, TP)

    def x_peer(d):
        return z * NX + lax.rem(x + d, NX)

    def remote(src, dst, send, recv, seq, tp):
        return pltpu.make_async_remote_copy(
            src_ref=src, dst_ref=dst, send_sem=send, recv_sem=recv,
            device_id=(seq, tp), device_id_type=MESH,
        )

    flight = []
    got = []

    def post(src, dst, send, recv, seq, tp):
        cp = remote(src, dst, send, recv, seq, tp)
        cp.start()
        flight.append(cp)
        return cp

    def land(cp):
        cp.wait_recv()
        got.append(id(cp))

    left_over = [0]

    def flush(count):
        for cp in flight[left_over[0] : count]:
            cp.wait_send()
        left_over[0] = count

    parity = lax.rem(x, 2)
    quarter = 2 * parity + x // 2
    loads = []

    def load(src, dst):
        cp = pltpu.make_async_copy(src, dst, ld.at[len(loads)])
        cp.start()
        loads.append(cp)
        return cp

    kept = 2 * parity + 1 - x // 2
    ld_frames = [
        load(frames.at[:, pl.ds(pl.multiple_of(q * 256, 256), 256)], xin.at[b])
        for b, q in enumerate((quarter, kept))
    ]

    bar = pltpu.get_barrier_semaphore()

    def far_first(n):
        return lax.rem(s + SEQ // 2 + ((n + 1) // 2) * (1 - 2 * lax.rem(n, 2)), SEQ)

    def greet(n, carry):
        pl.semaphore_signal(bar, inc=1, device_id=(far_first(n), t), device_id_type=MESH)
        return carry

    for d in (4, 5, 3, 6, 2, 7, 1):
        pl.semaphore_signal(bar, inc=1, device_id=(s, lax.rem(t + d, TP)), device_id_type=MESH)
    lax.fori_loop(0, SEQ - 1, greet, 0)

    ld_wo = load(wo, wof.at[pl.ds(pl.multiple_of(t * LW, LW), LW)])
    ld_map = load(smap_hbm, smap)
    ld_rec = [load(lens_hbm, lens), load(wins_hbm, wins)]
    ld_qkv = [
        load(gain1_hbm, gain1),
        load(wqkv.at[1], wkv.at[:, 0:LW]),
        load(wqkv.at[2], wkv.at[:, LW : 2 * LW]),
        load(wqkv.at[0], wq),
    ]
    ld_conv = [
        load(taps_hbm, taps), load(bn_scale_hbm, bn_scale), load(bn_shift_hbm, bn_shift)
    ]
    ld_w1 = [load(gain2_hbm, gain2), load(w1.at[0], w1v.at[:, 0:LW]), load(w1.at[1], w1v.at[:, LW : 2 * LW])]
    ld_w2 = load(
        w2.at[:, pl.ds(pl.multiple_of(t * LW, LW), LW)],
        w2c.at[pl.ds(pl.multiple_of(t * LW, LW), LW)],
    )

    for cp in ld_frames:
        cp.wait()
    o = iota((HALF, HALF), 0)
    pack = one_hot(iota((HALF, HALF), 1) == 64 * ((o >> 2) & 1) + 4 * (o >> 3) + (o & 3))
    for g in range(4):
        rows = slice(64 * g, 64 * g + 64)
        stack = jnp.concatenate(
            [
                jnp.concatenate([xin[b, rows, 0:128], xin[b, rows, 128:256]], axis=0)
                for b in range(2)
            ],
            axis=1,
        )
        packed = dot(pack, stack)
        for b in range(2):
            part = packed[:, 128 * b : 128 * b + 128].reshape(16, MSG, 128)
            sbuf[b, 16 * g : 16 * g + 16] = part.astype(BF16)

    pl.semaphore_wait(bar, SEQ - 1 + TP - 1)

    def wo_rows(tp, c):
        return wof.at[pl.ds(pl.multiple_of(tp * LW + c * 64, 64), 64)]

    def wo_block(tp, c, y):
        return wof.at[
            pl.ds(pl.multiple_of(tp * LW + c * 64, 64), 64), pl.ds(pl.multiple_of(y * LW, LW), LW)
        ]

    y = s // 8
    ld_wo.wait()
    part = wo_block(t, core, y)
    wo_cross = post(part, part, wos.at[3], wor.at[3], s, z_peer)
    wo_first = []
    for d in range(1, NX):
        part = wo_rows(t, core)
        wo_first.append(post(part, part, wos.at[d - 1], wor.at[d - 1], s, x_peer(d)))

    own = []
    deals = []
    for b in range(2):

        def deal(n, carry):
            j = far_first(n)
            remote(sbuf.at[b, j], rbuf.at[b, s], a2a_s.at[b], a2a_r.at[b], j, t).start()
            return carry

        lax.fori_loop(0, SEQ - 1, deal, 0)
        cp = pltpu.make_async_copy(sbuf.at[b, s], rbuf.at[b, s], own_sem.at[b])
        cp.start()
        own.append(cp)
        deals.append(
            remote(
                sbuf.at[b, 0 : SEQ - 1], rbuf.at[b, 0 : SEQ - 1], a2a_s.at[b], a2a_r.at[b], right, t
            )
        )

    ld_map.wait()
    col = dot_nt(one_hot(iota((8, SEQ), 1) == s), smap[...].astype(F32).astype(BF16))
    i = iota((8, SEQ * MSG), 1)
    spread = one_hot((iota((SEQ, SEQ * MSG), 1) >> 3) == iota((SEQ, SEQ * MSG), 0))
    place = dot(col.astype(BF16), spread) * 4.0 + (i & 3).astype(F32)
    o = iota((ROWS, SEQ * MSG), 0).astype(F32)
    for c in range(2):
        order[c] = one_hot(jnp.where(((i >> 2) & 1) == c, place, -1.0)[0:1, :] == o)

    for cp in ld_rec:
        cp.wait()
    pos = s * ROWS + iota((ROWS, LW), 0)
    start = jnp.zeros((ROWS, LW), I32)
    end = jnp.full((ROWS, LW), SEQ * ROWS, I32)
    reach = jnp.zeros((ROWS, LW), I32)
    total = jnp.int32(0)
    for k in range(8):
        before = total
        total = total + lens[k]
        start = jnp.where(pos >= total, total, start)
        end = jnp.where(pos < total, jnp.minimum(end, total), end)
        reach = jnp.where((pos >= before) & (pos < total), wins[k], reach)
    start_ref[...] = start
    end_ref[...] = end
    lo_ref[...] = jnp.maximum(start, pos - reach)
    hi_ref[...] = jnp.minimum(end - 1, pos + reach)

    def settle(b, q):
        own[b].wait()
        deals[b].wait_recv()
        dealt = rbuf[b].astype(F32).reshape(SEQ * MSG, 128).astype(BF16)
        for c in range(2):
            frame[q, :, 128 * c : 128 * c + 128] = dot(order[c], dealt).astype(BF16)

    land(wo_cross)
    part = wo_block(z_peer, core, y)
    wo_opposite = post(part, part, wos.at[4], wor.at[4], s, x_peer(2))

    settle(0, quarter)
    def half_rows(c, first=0, count=HALF):
        return pl.ds(pl.multiple_of(c * HALF + first, 64), count)

    FAR_NEAR = ((0, core, jnp.where(core == 0, left, right)), (1, 1 - core, mate))
    swaps = []
    for k, c, _ in FAR_NEAR:
        part = frame.at[quarter, half_rows(c)]
        swaps.append(
            [post(part, part, xs.at[k, n], xr.at[k, n], s, x_peer(d)) for n, d in enumerate((1, 3))]
        )
    settle(1, kept)

    def share(tp, first):
        part = wo_block(tp, core, y)
        return [
            post(part, part, wos.at[first + d], wor.at[first + d], lax.rem(s + 8 * d, SEQ), t)
            for d in (4, 3, 5, 2, 6, 1, 7)
        ]

    wo_share = share(z_peer, 13)

    def group_peer(k):
        return lax.rem(x_peer(k % NX) + k // NX * NX, TP)

    w2_first = {}

    def give_w2(steps):
        for k in steps:
            peer = group_peer(k)
            cols = pl.ds(pl.multiple_of(peer * LW, LW), LW)
            w2_first[k] = post(
                w2.at[pl.ds(pl.multiple_of(core * 64, 64), 64), cols],
                w2c.at[pl.ds(pl.multiple_of(t * LW + core * 64, 64), 64)],
                w2s.at[k - 1], w2r.at[k - 1], s, peer,
            )

    give_w2(range(NX, TP))

    for cp in ld_qkv:
        cp.wait()
    halos = []
    normed = []
    for k, c, peer in FAR_NEAR:
        for cp in swaps[k]:
            land(cp)
        z1 = layer_norm([frame[q, half_rows(c), :].astype(F32) for q in range(4)], gain1)
        normed.append(z1)
        here = half_rows(c, WMAX)
        kvx[here, :] = dot(z1, wkv[...]).astype(BF16)
        there = half_rows(3 * (1 - c))
        halos.append(post(kvx.at[here], kvx.at[there], hs.at[k], hr.at[k], peer, t))
    for k, c, _ in FAR_NEAR:
        qv[half_rows(c), :] = dot(normed[k], wq[...]).astype(BF16)

    for cp in wo_share:
        land(cp)
    wo_next = []
    for n, d in enumerate((1, 3)):
        part = wo_rows(z_peer, core)
        wo_next.append(post(part, part, wos.at[5 + n], wor.at[5 + n], s, x_peer(d)))
    wo_swap = []

    def give_wo(tp):
        k = 7 + len(wo_swap)
        cp = post(wo_rows(tp, core), wo_rows(tp, core), wos.at[k], wor.at[k], mate, t)
        wo_swap.append(cp)

    give_wo(z_peer)
    for d in range(1, NX):
        land(wo_first[d - 1])
        give_wo(x_peer(NX - d))

    x_peers = [x_peer(1), x_peer(2), x_peer(3)]

    def send_group(buf, rows, send, recv, peers, first):
        return [
            post(buf.at[t, rows], buf.at[t, rows], send.at[k], recv.at[k], s, peer)
            for k, peer in enumerate(peers, first)
        ]

    def pass_on(buf, rows, send, recv, sent):
        land(sent[0])
        for d in range(1, NX):
            cp = post(
                buf.at[z_peer, rows], buf.at[z_peer, rows], send.at[3 + d], recv.at[3 + d],
                s, x_peer(d),
            )
            sent.append(cp)

    def send_direct(buf, rows, send, recv):
        return [
            post(
                buf.at[t, rows], buf.at[t, rows], send.at[k], recv.at[k], s, lax.rem(t + d, TP)
            )
            for k, d in enumerate((4, 5, 3, 6, 2, 7, 1))
        ]

    def whole(buf, rows, sent):
        for cp in sent:
            if id(cp) not in got:
                land(cp)
        return jnp.concatenate([buf[k, rows, :] for k in range(TP)], axis=1)

    EDGES = (slice(192, 256), slice(0, 64))
    PLACES = (slice(0, HALF), slice(HALF, ROWS))
    BLOCKS = (slice(0, HALF), slice(HALF, ROWS))

    def natural(ref_rows, c):
        if c == 1:
            return ref_rows(slice(64, 192))
        return jnp.concatenate([ref_rows(e) for e in EDGES], axis=0)

    scale = 1.0 / math.sqrt(LW)

    def masked_scores(c, first, count):
        rows = half_rows(c)
        scores = dot_nt(qv[rows, :], kvx[pl.ds(first, count), 0:LW]) * scale
        kpos = s * ROWS + first - WMAX + iota((HALF, count), 1)
        low = jnp.concatenate([lo_ref[rows, :]] * (count // LW), axis=1)
        high = jnp.concatenate([hi_ref[rows, :]] * (count // LW), axis=1)
        return jnp.where((kpos >= low) & (kpos <= high), scores, -1e30)

    def attend_own(c):
        scores = masked_scores(c, WMAX, ROWS)
        peak = jnp.max(scores, axis=1, keepdims=True)
        weights = jnp.exp(scores - peak)
        total = jnp.sum(weights, axis=1, keepdims=True)
        return peak, total, dot(weights.astype(BF16), kvx[WMAX : WMAX + ROWS, LW : 2 * LW])

    own_part = [attend_own(c) for _, c, _ in FAR_NEAR]
    for k in (1, 0):
        c = FAR_NEAR[k][1]
        first = pl.multiple_of(c * (WMAX + ROWS), HALF)
        land(halos[k])
        scores = masked_scores(c, first, WMAX)
        own_peak, own_total, own_sum = own_part[k]
        peak = jnp.maximum(own_peak, jnp.max(scores, axis=1, keepdims=True))
        weights = jnp.exp(scores - peak)
        fade = jnp.exp(own_peak - peak)
        total = own_total * fade + jnp.sum(weights, axis=1, keepdims=True)
        mixed = own_sum * fade + dot(weights.astype(BF16), kvx[pl.ds(first, WMAX), LW : 2 * LW])
        mixed = (mixed / total).astype(BF16)
        ctx[t, half_rows(c, 64, 64), :] = mixed[0:64]
        ctx[t, half_rows(1 - c, 0, 64), :] = mixed[64:128]
    posted = len(flight)
    sent1 = {}
    for c in (0, 1):
        sent1[c] = send_group(ctx, PLACES[c], c1s.at[c], c1r.at[c], [z_peer], 0)
    for c in (0, 1):
        sent1[c] += send_group(ctx, PLACES[c], c1s.at[c], c1r.at[c], x_peers, 1)

    z_opposite = lax.rem(x_peer(2) + NX, TP)
    land(wo_opposite)
    wo_share_opposite = share(z_opposite, 20)
    for cp in deals:
        cp.wait_send()
    flush(posted)

    for n, d in enumerate((1, 3)):
        land(wo_next[n])
        give_wo(lax.rem(x_peer(NX - d) + NX, TP))
    for c in (0, 1):
        pass_on(ctx, PLACES[c], c1s.at[c], c1r.at[c], sent1[c])

    give_w2(range(1, NX))

    for cp in wo_share_opposite:
        land(cp)
    give_wo(z_opposite)
    for cp in wo_swap:
        land(cp)
    for cp in ld_w1:
        cp.wait()

    def conv_act(first, count):
        rows = slice(first, first + count)
        at = s * ROWS + first + iota((count, LW), 0)
        room_low = start_ref[rows, :] - at
        room_high = end_ref[rows, :] - at
        conv = jnp.zeros((count, LW), F32)
        for k in range(TAPS):
            begin = EDGE + first + k - RIM
            valid = (room_low <= k - RIM) & (room_high > k - RIM)
            conv = conv + jnp.where(valid, gluf[begin : begin + count, :] * taps[k : k + 1, :], 0.0)
        shifted = conv * bn_scale[...] + bn_shift[...]
        return (shifted * jax.nn.sigmoid(shifted)).astype(BF16)

    edges = []
    for c in (0, 1):
        attn = dot(whole(ctx, BLOCKS[c], sent1[c]), wof[...])
        resid = [
            (
                natural(lambda rows: frame[q, rows, :], c).astype(F32)
                + attn[:, 256 * q : 256 * q + 256]
            ).astype(BF16)
            for q in range(4)
        ]
        for q in range(4):
            for half in range(2):
                part = resid[q][:, half * LW : (half + 1) * LW]
                if c == 0:
                    res[2 * q + half, 192:256, :] = part[0:64]
                    res[2 * q + half, 0:64, :] = part[64:128]
                else:
                    res[2 * q + half, 64:192, :] = part
        z2 = layer_norm([r.astype(F32) for r in resid], gain2)
        both = dot(z2, w1v[...])
        gated = (both[:, 0:LW] * jax.nn.sigmoid(both[:, LW : 2 * LW])).astype(BF16)
        if c == 0:
            glu[0] = gated[64 - EDGE : 64]
            glu[1] = gated[64 : 64 + EDGE]
            edges.append(post(glu.at[0], rim.at[0], gs.at[0], gr.at[0], right, t))
            edges.append(post(glu.at[1], rim.at[1], gs.at[1], gr.at[1], left, t))
            gluf[EDGE + 192 : EDGE + 256, :] = gated[0:64].astype(F32)
            gluf[EDGE : EDGE + 64, :] = gated[64:128].astype(F32)
        else:
            gluf[EDGE + 64 : EDGE + 192, :] = gated.astype(F32)

    for cp in ld_conv:
        cp.wait()
    PIECES = ((0, 80), (80, 160), (160, 224))
    posted = len(flight)
    sent2 = []
    for n, (begin, stop) in enumerate(PIECES):
        act[t, begin:stop, :] = conv_act(EDGE + begin, stop - begin)
        sent2.append(
            send_group(act, slice(begin, stop), c2s.at[n], c2r.at[n], [z_peer], 0)
        )
    for n, (begin, stop) in enumerate(PIECES):
        sent2[n] += send_group(act, slice(begin, stop), c2s.at[n], c2r.at[n], x_peers, 1)
    land(edges[0])
    gluf[0:EDGE, :] = rim[0].astype(F32)
    land(edges[1])
    gluf[EDGE + ROWS : 2 * EDGE + ROWS, :] = rim[1].astype(F32)
    act[t, 224:240, :] = conv_act(ROWS - EDGE, EDGE)
    act[t, 240:256, :] = conv_act(0, EDGE)
    last = send_direct(act, slice(224, 256), c2s.at[3], c2r.at[3])
    flush(posted)

    w2_swap = []
    for k in (4, 5, 6, 7, 1, 2, 3):
        land(w2_first[k])
        source = group_peer(k // NX * NX + (NX - k) % NX)
        part = w2c.at[pl.ds(pl.multiple_of(source * LW + core * 64, 64), 64)]
        w2_swap.append(post(part, part, w2s.at[6 + k], w2r.at[6 + k], mate, t))
    posted = len(flight)
    for n, (begin, stop) in enumerate(PIECES):
        pass_on(act, slice(begin, stop), c2s.at[n], c2r.at[n], sent2[n])
    ld_w2.wait()
    for cp in w2_swap:
        land(cp)
    flush(posted)

    def finish(first, count, begin, sent):
        summed = dot(whole(act, slice(begin, begin + count), sent), w2c[...])
        rows = slice(first, first + count)
        outv[rows, :] = (res[t, rows, :].astype(F32) + summed).astype(BF16)

    for n, (begin, stop) in enumerate(PIECES):
        finish(EDGE + begin, stop - begin, begin, sent2[n])
    finish(ROWS - EDGE, EDGE, 224, last)
    finish(0, EDGE, 240, last)
    cp = pltpu.make_async_copy(outv, out, out_sem)
    cp.start()
    flush(len(flight))
    cp.wait()


def local(
    frames_in, stretch_map, rec_lengths, windows, ln1_gain, wqkv, wo, ln2_gain, w1,
    dw_kernel, bn_scale, bn_shift, w2,
):
    hbm = pl.BlockSpec(memory_space=pl.ANY)
    dma = pltpu.SemaphoreType.DMA
    return pl.pallas_call(
        block_kernel,
        out_shape=jax.ShapeDtypeStruct((ROWS, LW), BF16),
        in_specs=[hbm] * 13,
        out_specs=hbm,
        scratch_shapes=[
            pltpu.VMEM((SEQ, SEQ), I32),
            pltpu.SMEM((8,), I32),
            pltpu.SMEM((8,), I32),
            pltpu.VMEM((1, D), F32),
            pltpu.VMEM((1, D), F32),
            pltpu.VMEM((TAPS, LW), F32),
            pltpu.VMEM((1, LW), F32),
            pltpu.VMEM((1, LW), F32),
            pltpu.VMEM((ROWS, LW), BF16),
            pltpu.VMEM((2, ROWS, 256), BF16),
            pltpu.VMEM((2, SEQ, MSG, 128), BF16),
            pltpu.VMEM((2, SEQ, MSG, 128), BF16),
            pltpu.VMEM((2, ROWS, SEQ * MSG), BF16),
            pltpu.VMEM((4, ROWS, 256), BF16),
            pltpu.VMEM((D, LW), BF16),
            pltpu.VMEM((D, 2 * LW), BF16),
            pltpu.VMEM((D, 2 * LW), BF16),
            pltpu.VMEM((D, D), BF16),
            pltpu.VMEM((D, LW), BF16),
            pltpu.VMEM((ROWS, LW), BF16),
            pltpu.VMEM((ROWS + 2 * WMAX, 2 * LW), BF16),
            pltpu.VMEM((TP, ROWS, LW), BF16),
            pltpu.VMEM((TP, ROWS, LW), BF16),
            pltpu.VMEM((TP, ROWS, LW), BF16),
            pltpu.VMEM((2, EDGE, LW), BF16),
            pltpu.VMEM((ROWS + 2 * EDGE, LW), F32),
            pltpu.VMEM((2, EDGE, LW), BF16),
            pltpu.VMEM((ROWS, LW), I32),
            pltpu.VMEM((ROWS, LW), I32),
            pltpu.VMEM((ROWS, LW), I32),
            pltpu.VMEM((ROWS, LW), I32),
            dma((17,)),
            dma,
            dma((2,)),
            dma((2,)),
            dma((2,)),
            dma((2, 2)),
            dma((2, 2)),
            dma((2,)),
            dma((2,)),
            dma((28,)),
            dma((28,)),
            dma((14,)),
            dma((14,)),
            dma((3, 7)),
            dma((3, 7)),
            dma((4, 7)),
            dma((4, 7)),
            dma((2,)),
            dma((2,)),
        ],
        compiler_params=pltpu.CompilerParams(
            collective_id=0, has_side_effects=True, vmem_limit_bytes=60 << 20
        ),
        name="encoder_block",
    )(
        frames_in, stretch_map, rec_lengths, windows, ln1_gain.reshape(1, D), wqkv, wo,
        ln2_gain.reshape(1, D), w1, dw_kernel, bn_scale.reshape(1, LW),
        bn_shift.reshape(1, LW), w2,
    )


def solution(mesh):
    placed = (
        P("seq", None),
        P(),
        P(),
        P(),
        P(),
        P(None, None, "tp"),
        P("tp", None),
        P(),
        P(None, None, "tp"),
        P(None, "tp"),
        P("tp"),
        P("tp"),
        P("tp", None),
    )
    return jax.shard_map(
        local, mesh=mesh, in_specs=placed, out_specs=P("seq", "tp"), check_vma=False
    )
```

```python
import functools
import math

import jax
import jax.numpy as jnp
from jax import lax
from jax.experimental import pallas as pl
from jax.experimental.pallas import tpu as pltpu
from jax.sharding import PartitionSpec as P

MESH = pl.DeviceIdType.MESH
BF16 = jnp.bfloat16
F32 = jnp.float32
I32 = jnp.int32

SEQ = 64
TP = 8
NX = 4
ROWS = 256
HALF = 128
D = 1024
LW = 128
PIECE = 4
MSG = 8
WMAX = 128
TAPS = 9
RIM = 4
EDGE = 16


def dot(a, b):
    return jnp.dot(a, b, preferred_element_type=F32)


def dot_nt(a, b):
    return lax.dot_general(a, b, (((1,), (1,)), ((), ())), preferred_element_type=F32)


def iota(shape, dim):
    return lax.broadcasted_iota(I32, shape, dim)


def one_hot(mask):
    return jnp.where(mask, 1.0, 0.0).astype(BF16)


def layer_norm(blocks, gain_ref):
    width = blocks[0].shape[1]
    mean = sum(jnp.sum(b, axis=1, keepdims=True) for b in blocks) * (1.0 / D)
    centred = [b - mean for b in blocks]
    var = sum(jnp.sum(c * c, axis=1, keepdims=True) for c in centred) * (1.0 / D)
    inv = lax.rsqrt(var + 1e-05)
    normed = [
        (c * inv * gain_ref[:, i * width : (i + 1) * width]).astype(BF16)
        for i, c in enumerate(centred)
    ]
    return jnp.concatenate(normed, axis=1)


def block_kernel(
    frames, smap_hbm, lens_hbm, wins_hbm, gain1_hbm, wqkv, wo, gain2_hbm, w1, taps_hbm,
    bn_scale_hbm, bn_shift_hbm, w2,
    out,
    smap, lens, wins, gain1, gain2, taps, bn_scale, bn_shift,
    outv, xin, sbuf, rbuf, order, frame, wq, wkv, w1v, wof, w2c, qv, kvx, ctx, act, res, glu, gluf, rim,
    lo_ref, hi_ref, start_ref, end_ref,
    ld, out_sem, own_sem, a2a_s, a2a_r, xs, xr, hs, hr, wos, wor, w2s, w2r, c1s, c1r, c2s, c2r, gs, gr,
):
    s = lax.axis_index("seq")
    t = lax.axis_index("tp")
    z = t // NX
    x = lax.rem(t, NX)
    core = lax.rem(s, 2)
    mate = s + 1 - 2 * core
    left = lax.rem(s + SEQ - 1, SEQ)
    right = lax.rem(s + 1, SEQ)
    z_peer = lax.rem(t + NX, TP)

    def x_peer(d):
        return z * NX + lax.rem(x + d, NX)

    def remote(src, dst, send, recv, seq, tp):
        return pltpu.make_async_remote_copy(
            src_ref=src, dst_ref=dst, send_sem=send, recv_sem=recv,
            device_id=(seq, tp), device_id_type=MESH,
        )

    flight = []
    got = []

    def post(src, dst, send, recv, seq, tp):
        cp = remote(src, dst, send, recv, seq, tp)
        cp.start()
        flight.append(cp)
        return cp

    def land(cp):
        cp.wait_recv()
        got.append(id(cp))

    left_over = [0]

    def flush(count):
        for cp in flight[left_over[0] : count]:
            cp.wait_send()
        left_over[0] = count

    parity = lax.rem(x, 2)
    quarter = 2 * parity + x // 2
    loads = []

    def load(src, dst):
        cp = pltpu.make_async_copy(src, dst, ld.at[len(loads)])
        cp.start()
        loads.append(cp)
        return cp

    kept = 2 * parity + 1 - x // 2
    ld_frames = [
        load(frames.at[:, pl.ds(pl.multiple_of(q * 256, 256), 256)], xin.at[b])
        for b, q in enumerate((quarter, kept))
    ]

    bar = pltpu.get_barrier_semaphore()

    def far_first(n):
        return lax.rem(s + SEQ // 2 + ((n + 1) // 2) * (1 - 2 * lax.rem(n, 2)), SEQ)

    def greet(n, carry):
        pl.semaphore_signal(bar, inc=1, device_id=(far_first(n), t), device_id_type=MESH)
        return carry

    for d in (4, 5, 3, 6, 2, 7, 1):
        pl.semaphore_signal(bar, inc=1, device_id=(s, lax.rem(t + d, TP)), device_id_type=MESH)
    lax.fori_loop(0, SEQ - 1, greet, 0)

    ld_wo = load(wo, wof.at[pl.ds(pl.multiple_of(t * LW, LW), LW)])
    ld_map = load(smap_hbm, smap)
    ld_rec = [load(lens_hbm, lens), load(wins_hbm, wins)]
    ld_qkv = [
        load(gain1_hbm, gain1),
        load(wqkv.at[1], wkv.at[:, 0:LW]),
        load(wqkv.at[2], wkv.at[:, LW : 2 * LW]),
        load(wqkv.at[0], wq),
    ]
    ld_conv = [
        load(taps_hbm, taps), load(bn_scale_hbm, bn_scale), load(bn_shift_hbm, bn_shift)
    ]
    ld_w1 = [load(gain2_hbm, gain2), load(w1.at[0], w1v.at[:, 0:LW]), load(w1.at[1], w1v.at[:, LW : 2 * LW])]
    ld_w2 = load(
        w2.at[:, pl.ds(pl.multiple_of(t * LW, LW), LW)],
        w2c.at[pl.ds(pl.multiple_of(t * LW, LW), LW)],
    )

    for cp in ld_frames:
        cp.wait()
    o = iota((HALF, HALF), 0)
    pack = one_hot(iota((HALF, HALF), 1) == 64 * ((o >> 2) & 1) + 4 * (o >> 3) + (o & 3))
    for g in range(4):
        rows = slice(64 * g, 64 * g + 64)
        stack = jnp.concatenate(
            [
                jnp.concatenate([xin[b, rows, 0:128], xin[b, rows, 128:256]], axis=0)
                for b in range(2)
            ],
            axis=1,
        )
        packed = dot(pack, stack)
        for b in range(2):
            part = packed[:, 128 * b : 128 * b + 128].reshape(16, MSG, 128)
            sbuf[b, 16 * g : 16 * g + 16] = part.astype(BF16)

    pl.semaphore_wait(bar, SEQ - 1 + TP - 1)

    def wo_rows(tp, c):
        return wof.at[pl.ds(pl.multiple_of(tp * LW + c * 64, 64), 64)]

    def wo_block(tp, c, y):
        return wof.at[
            pl.ds(pl.multiple_of(tp * LW + c * 64, 64), 64), pl.ds(pl.multiple_of(y * LW, LW), LW)
        ]

    y = s // 8
    ld_wo.wait()
    part = wo_block(t, core, y)
    wo_cross = post(part, part, wos.at[3], wor.at[3], s, z_peer)
    wo_first = []
    for d in range(1, NX):
        part = wo_rows(t, core)
        wo_first.append(post(part, part, wos.at[d - 1], wor.at[d - 1], s, x_peer(d)))

    own = []
    deals = []
    for b in range(2):

        def deal(n, carry):
            j = far_first(n)
            remote(sbuf.at[b, j], rbuf.at[b, s], a2a_s.at[b], a2a_r.at[b], j, t).start()
            return carry

        lax.fori_loop(0, SEQ - 1, deal, 0)
        cp = pltpu.make_async_copy(sbuf.at[b, s], rbuf.at[b, s], own_sem.at[b])
        cp.start()
        own.append(cp)
        deals.append(
            remote(
                sbuf.at[b, 0 : SEQ - 1], rbuf.at[b, 0 : SEQ - 1], a2a_s.at[b], a2a_r.at[b], right, t
            )
        )

    ld_map.wait()
    col = dot_nt(one_hot(iota((8, SEQ), 1) == s), smap[...].astype(F32).astype(BF16))
    i = iota((8, SEQ * MSG), 1)
    spread = one_hot((iota((SEQ, SEQ * MSG), 1) >> 3) == iota((SEQ, SEQ * MSG), 0))
    place = dot(col.astype(BF16), spread) * 4.0 + (i & 3).astype(F32)
    o = iota((ROWS, SEQ * MSG), 0).astype(F32)
    for c in range(2):
        order[c] = one_hot(jnp.where(((i >> 2) & 1) == c, place, -1.0)[0:1, :] == o)

    for cp in ld_rec:
        cp.wait()
    pos = s * ROWS + iota((ROWS, LW), 0)
    start = jnp.zeros((ROWS, LW), I32)
    end = jnp.full((ROWS, LW), SEQ * ROWS, I32)
    reach = jnp.zeros((ROWS, LW), I32)
    total = jnp.int32(0)
    for k in range(8):
        before = total
        total = total + lens[k]
        start = jnp.where(pos >= total, total, start)
        end = jnp.where(pos < total, jnp.minimum(end, total), end)
        reach = jnp.where((pos >= before) & (pos < total), wins[k], reach)
    start_ref[...] = start
    end_ref[...] = end
    lo_ref[...] = jnp.maximum(start, pos - reach)
    hi_ref[...] = jnp.minimum(end - 1, pos + reach)

    def settle(b, q):
        own[b].wait()
        deals[b].wait_recv()
        dealt = rbuf[b].astype(F32).reshape(SEQ * MSG, 128).astype(BF16)
        for c in range(2):
            frame[q, :, 128 * c : 128 * c + 128] = dot(order[c], dealt).astype(BF16)

    land(wo_cross)
    part = wo_block(z_peer, core, y)
    wo_opposite = post(part, part, wos.at[4], wor.at[4], s, x_peer(2))

    settle(0, quarter)
    def half_rows(c, first=0, count=HALF):
        return pl.ds(pl.multiple_of(c * HALF + first, 64), count)

    FAR_NEAR = ((0, core, jnp.where(core == 0, left, right)), (1, 1 - core, mate))
    swaps = []
    for k, c, _ in FAR_NEAR:
        part = frame.at[quarter, half_rows(c)]
        swaps.append(
            [post(part, part, xs.at[k, n], xr.at[k, n], s, x_peer(d)) for n, d in enumerate((1, 3))]
        )
    settle(1, kept)

    def share(tp, first):
        part = wo_block(tp, core, y)
        return [
            post(part, part, wos.at[first + d], wor.at[first + d], lax.rem(s + 8 * d, SEQ), t)
            for d in (4, 3, 5, 2, 6, 1, 7)
        ]

    wo_share = share(z_peer, 13)

    def group_peer(k):
        return lax.rem(x_peer(k % NX) + k // NX * NX, TP)

    w2_first = {}

    def give_w2(steps):
        for k in steps:
            peer = group_peer(k)
            cols = pl.ds(pl.multiple_of(peer * LW, LW), LW)
            w2_first[k] = post(
                w2.at[pl.ds(pl.multiple_of(core * 64, 64), 64), cols],
                w2c.at[pl.ds(pl.multiple_of(t * LW + core * 64, 64), 64)],
                w2s.at[k - 1], w2r.at[k - 1], s, peer,
            )

    give_w2(range(NX, TP))

    for cp in ld_qkv:
        cp.wait()
    halos = []
    normed = []
    for k, c, peer in FAR_NEAR:
        for cp in swaps[k]:
            land(cp)
        z1 = layer_norm([frame[q, half_rows(c), :].astype(F32) for q in range(4)], gain1)
        normed.append(z1)
        here = half_rows(c, WMAX)
        kvx[here, :] = dot(z1, wkv[...]).astype(BF16)
        there = half_rows(3 * (1 - c))
        halos.append(post(kvx.at[here], kvx.at[there], hs.at[k], hr.at[k], peer, t))
    for k, c, _ in FAR_NEAR:
        qv[half_rows(c), :] = dot(normed[k], wq[...]).astype(BF16)

    for cp in wo_share:
        land(cp)
    wo_next = []
    for n, d in enumerate((1, 3)):
        part = wo_rows(z_peer, core)
        wo_next.append(post(part, part, wos.at[5 + n], wor.at[5 + n], s, x_peer(d)))
    wo_swap = []

    def give_wo(tp):
        k = 7 + len(wo_swap)
        cp = post(wo_rows(tp, core), wo_rows(tp, core), wos.at[k], wor.at[k], mate, t)
        wo_swap.append(cp)

    give_wo(z_peer)
    for d in range(1, NX):
        land(wo_first[d - 1])
        give_wo(x_peer(NX - d))

    x_peers = [x_peer(1), x_peer(2), x_peer(3)]

    def send_group(buf, rows, send, recv, peers, first):
        return [
            post(buf.at[t, rows], buf.at[t, rows], send.at[k], recv.at[k], s, peer)
            for k, peer in enumerate(peers, first)
        ]

    def pass_on(buf, rows, send, recv, sent):
        land(sent[0])
        for d in range(1, NX):
            cp = post(
                buf.at[z_peer, rows], buf.at[z_peer, rows], send.at[3 + d], recv.at[3 + d],
                s, x_peer(d),
            )
            sent.append(cp)

    def send_direct(buf, rows, send, recv):
        return [
            post(
                buf.at[t, rows], buf.at[t, rows], send.at[k], recv.at[k], s, lax.rem(t + d, TP)
            )
            for k, d in enumerate((4, 5, 3, 6, 2, 7, 1))
        ]

    def whole(buf, rows, sent):
        for cp in sent:
            if id(cp) not in got:
                land(cp)
        return jnp.concatenate([buf[k, rows, :] for k in range(TP)], axis=1)

    EDGES = (slice(192, 256), slice(0, 64))
    PLACES = (slice(0, HALF), slice(HALF, ROWS))
    BLOCKS = (slice(0, HALF), slice(HALF, ROWS))

    def natural(ref_rows, c):
        if c == 1:
            return ref_rows(slice(64, 192))
        return jnp.concatenate([ref_rows(e) for e in EDGES], axis=0)

    scale = 1.0 / math.sqrt(LW)

    def masked_scores(c, first, count):
        rows = half_rows(c)
        scores = dot_nt(qv[rows, :], kvx[pl.ds(first, count), 0:LW]) * scale
        kpos = s * ROWS + first - WMAX + iota((HALF, count), 1)
        low = jnp.concatenate([lo_ref[rows, :]] * (count // LW), axis=1)
        high = jnp.concatenate([hi_ref[rows, :]] * (count // LW), axis=1)
        return jnp.where((kpos >= low) & (kpos <= high), scores, -1e30)

    def attend_own(c):
        scores = masked_scores(c, WMAX, ROWS)
        peak = jnp.max(scores, axis=1, keepdims=True)
        weights = jnp.exp(scores - peak)
        total = jnp.sum(weights, axis=1, keepdims=True)
        return peak, total, dot(weights.astype(BF16), kvx[WMAX : WMAX + ROWS, LW : 2 * LW])

    own_part = [attend_own(c) for _, c, _ in FAR_NEAR]
    for k in (1, 0):
        c = FAR_NEAR[k][1]
        first = pl.multiple_of(c * (WMAX + ROWS), HALF)
        land(halos[k])
        scores = masked_scores(c, first, WMAX)
        own_peak, own_total, own_sum = own_part[k]
        peak = jnp.maximum(own_peak, jnp.max(scores, axis=1, keepdims=True))
        weights = jnp.exp(scores - peak)
        fade = jnp.exp(own_peak - peak)
        total = own_total * fade + jnp.sum(weights, axis=1, keepdims=True)
        mixed = own_sum * fade + dot(weights.astype(BF16), kvx[pl.ds(first, WMAX), LW : 2 * LW])
        mixed = (mixed / total).astype(BF16)
        ctx[t, half_rows(c, 64, 64), :] = mixed[0:64]
        ctx[t, half_rows(1 - c, 0, 64), :] = mixed[64:128]
    posted = len(flight)
    sent1 = {}
    for c in (0, 1):
        sent1[c] = send_group(ctx, PLACES[c], c1s.at[c], c1r.at[c], [z_peer], 0)
    for c in (0, 1):
        sent1[c] += send_group(ctx, PLACES[c], c1s.at[c], c1r.at[c], x_peers, 1)

    z_opposite = lax.rem(x_peer(2) + NX, TP)
    land(wo_opposite)
    wo_share_opposite = share(z_opposite, 20)
    for cp in deals:
        cp.wait_send()
    flush(posted)

    pass_on(ctx, PLACES[0], c1s.at[0], c1r.at[0], sent1[0])
    for n, d in enumerate((1, 3)):
        land(wo_next[n])
        give_wo(lax.rem(x_peer(NX - d) + NX, TP))
    pass_on(ctx, PLACES[1], c1s.at[1], c1r.at[1], sent1[1])

    for cp in wo_share_opposite:
        land(cp)
    give_wo(z_opposite)
    for cp in wo_swap:
        land(cp)
    for cp in ld_w1:
        cp.wait()

    def conv_act(first, count):
        rows = slice(first, first + count)
        at = s * ROWS + first + iota((count, LW), 0)
        room_low = start_ref[rows, :] - at
        room_high = end_ref[rows, :] - at
        conv = jnp.zeros((count, LW), F32)
        for k in range(TAPS):
            begin = EDGE + first + k - RIM
            valid = (room_low <= k - RIM) & (room_high > k - RIM)
            conv = conv + jnp.where(valid, gluf[begin : begin + count, :] * taps[k : k + 1, :], 0.0)
        shifted = conv * bn_scale[...] + bn_shift[...]
        return (shifted * jax.nn.sigmoid(shifted)).astype(BF16)

    edges = []
    for c in (0, 1):
        gathered = whole(ctx, BLOCKS[c], sent1[c])
        if c == 1:
            give_w2(range(1, NX))
        attn = dot(gathered, wof[...])
        resid = [
            (
                natural(lambda rows: frame[q, rows, :], c).astype(F32)
                + attn[:, 256 * q : 256 * q + 256]
            ).astype(BF16)
            for q in range(4)
        ]
        for q in range(4):
            for half in range(2):
                part = resid[q][:, half * LW : (half + 1) * LW]
                if c == 0:
                    res[2 * q + half, 192:256, :] = part[0:64]
                    res[2 * q + half, 0:64, :] = part[64:128]
                else:
                    res[2 * q + half, 64:192, :] = part
        z2 = layer_norm([r.astype(F32) for r in resid], gain2)
        both = dot(z2, w1v[...])
        gated = (both[:, 0:LW] * jax.nn.sigmoid(both[:, LW : 2 * LW])).astype(BF16)
        if c == 0:
            glu[0] = gated[64 - EDGE : 64]
            glu[1] = gated[64 : 64 + EDGE]
            edges.append(post(glu.at[0], rim.at[0], gs.at[0], gr.at[0], right, t))
            edges.append(post(glu.at[1], rim.at[1], gs.at[1], gr.at[1], left, t))
            gluf[EDGE + 192 : EDGE + 256, :] = gated[0:64].astype(F32)
            gluf[EDGE : EDGE + 64, :] = gated[64:128].astype(F32)
        else:
            gluf[EDGE + 64 : EDGE + 192, :] = gated.astype(F32)

    for cp in ld_conv:
        cp.wait()
    PIECES = ((0, 80), (80, 160), (160, 224))
    posted = len(flight)
    sent2 = []
    for n, (begin, stop) in enumerate(PIECES):
        act[t, begin:stop, :] = conv_act(EDGE + begin, stop - begin)
        sent2.append(
            send_group(act, slice(begin, stop), c2s.at[n], c2r.at[n], [z_peer], 0)
        )
    for n, (begin, stop) in enumerate(PIECES):
        sent2[n] += send_group(act, slice(begin, stop), c2s.at[n], c2r.at[n], x_peers, 1)
    land(edges[0])
    gluf[0:EDGE, :] = rim[0].astype(F32)
    land(edges[1])
    gluf[EDGE + ROWS : 2 * EDGE + ROWS, :] = rim[1].astype(F32)
    act[t, 224:240, :] = conv_act(ROWS - EDGE, EDGE)
    act[t, 240:256, :] = conv_act(0, EDGE)
    last = send_direct(act, slice(224, 256), c2s.at[3], c2r.at[3])
    flush(posted)

    w2_swap = []
    for k in (4, 5, 6, 7, 1, 2, 3):
        land(w2_first[k])
        source = group_peer(k // NX * NX + (NX - k) % NX)
        part = w2c.at[pl.ds(pl.multiple_of(source * LW + core * 64, 64), 64)]
        w2_swap.append(post(part, part, w2s.at[6 + k], w2r.at[6 + k], mate, t))
    posted = len(flight)
    for n, (begin, stop) in enumerate(PIECES):
        pass_on(act, slice(begin, stop), c2s.at[n], c2r.at[n], sent2[n])
    ld_w2.wait()
    for cp in w2_swap:
        land(cp)
    flush(posted)

    def finish(first, count, begin, sent):
        summed = dot(whole(act, slice(begin, begin + count), sent), w2c[...])
        rows = slice(first, first + count)
        outv[rows, :] = (res[t, rows, :].astype(F32) + summed).astype(BF16)

    for n, (begin, stop) in enumerate(PIECES):
        finish(EDGE + begin, stop - begin, begin, sent2[n])
    finish(ROWS - EDGE, EDGE, 224, last)
    finish(0, EDGE, 240, last)
    cp = pltpu.make_async_copy(outv, out, out_sem)
    cp.start()
    flush(len(flight))
    cp.wait()


def local(
    frames_in, stretch_map, rec_lengths, windows, ln1_gain, wqkv, wo, ln2_gain, w1,
    dw_kernel, bn_scale, bn_shift, w2,
):
    hbm = pl.BlockSpec(memory_space=pl.ANY)
    dma = pltpu.SemaphoreType.DMA
    return pl.pallas_call(
        block_kernel,
        out_shape=jax.ShapeDtypeStruct((ROWS, LW), BF16),
        in_specs=[hbm] * 13,
        out_specs=hbm,
        scratch_shapes=[
            pltpu.VMEM((SEQ, SEQ), I32),
            pltpu.SMEM((8,), I32),
            pltpu.SMEM((8,), I32),
            pltpu.VMEM((1, D), F32),
            pltpu.VMEM((1, D), F32),
            pltpu.VMEM((TAPS, LW), F32),
            pltpu.VMEM((1, LW), F32),
            pltpu.VMEM((1, LW), F32),
            pltpu.VMEM((ROWS, LW), BF16),
            pltpu.VMEM((2, ROWS, 256), BF16),
            pltpu.VMEM((2, SEQ, MSG, 128), BF16),
            pltpu.VMEM((2, SEQ, MSG, 128), BF16),
            pltpu.VMEM((2, ROWS, SEQ * MSG), BF16),
            pltpu.VMEM((4, ROWS, 256), BF16),
            pltpu.VMEM((D, LW), BF16),
            pltpu.VMEM((D, 2 * LW), BF16),
            pltpu.VMEM((D, 2 * LW), BF16),
            pltpu.VMEM((D, D), BF16),
            pltpu.VMEM((D, LW), BF16),
            pltpu.VMEM((ROWS, LW), BF16),
            pltpu.VMEM((ROWS + 2 * WMAX, 2 * LW), BF16),
            pltpu.VMEM((TP, ROWS, LW), BF16),
            pltpu.VMEM((TP, ROWS, LW), BF16),
            pltpu.VMEM((TP, ROWS, LW), BF16),
            pltpu.VMEM((2, EDGE, LW), BF16),
            pltpu.VMEM((ROWS + 2 * EDGE, LW), F32),
            pltpu.VMEM((2, EDGE, LW), BF16),
            pltpu.VMEM((ROWS, LW), I32),
            pltpu.VMEM((ROWS, LW), I32),
            pltpu.VMEM((ROWS, LW), I32),
            pltpu.VMEM((ROWS, LW), I32),
            dma((17,)),
            dma,
            dma((2,)),
            dma((2,)),
            dma((2,)),
            dma((2, 2)),
            dma((2, 2)),
            dma((2,)),
            dma((2,)),
            dma((28,)),
            dma((28,)),
            dma((14,)),
            dma((14,)),
            dma((3, 7)),
            dma((3, 7)),
            dma((4, 7)),
            dma((4, 7)),
            dma((2,)),
            dma((2,)),
        ],
        compiler_params=pltpu.CompilerParams(
            collective_id=0, has_side_effects=True, vmem_limit_bytes=60 << 20
        ),
        name="encoder_block",
    )(
        frames_in, stretch_map, rec_lengths, windows, ln1_gain.reshape(1, D), wqkv, wo,
        ln2_gain.reshape(1, D), w1, dw_kernel, bn_scale.reshape(1, LW),
        bn_shift.reshape(1, LW), w2,
    )


def solution(mesh):
    placed = (
        P("seq", None),
        P(),
        P(),
        P(),
        P(),
        P(None, None, "tp"),
        P("tp", None),
        P(),
        P(None, None, "tp"),
        P(None, "tp"),
        P("tp"),
        P("tp"),
        P("tp", None),
    )
    return jax.shard_map(
        local, mesh=mesh, in_specs=placed, out_specs=P("seq", "tp"), check_vma=False
    )
```
